32 devices in a mesh: groups: 2 (over y), ctx: 4 (over z), dp: 4 (over x, core).
Axes of the slice: x: 2, y: 2, z: 4, core: 2. Of those that a mesh axis runs over, the one named last changes fastest.
Arguments:
- values: bfloat16 [8, 512, 1024], P(('groups', 'dp'), 'ctx'), parts along dimension 0, may hold values from -6 to 6
- grads_out: bfloat16 [8, 512, 1024], P(('groups', 'dp'), 'ctx'), parts along dimension 0, may hold values from -6 to 6
- w_first: float32 [5, 64], replicated, may hold values from -2.5 to 2.5
- sine_freq: float32 [64], replicated, may hold values from 0.5 to 2
- w_inner: float32 [64, 64], replicated, may hold values from -0.75 to 0.75
- w_last: float32 [64, 1024], replicated, may hold values from -0.75 to 0.75
- decay_rates: float32 [1024], replicated, may hold values from 6e-05 to 0.03
Outputs:
- grad_first: float32 [10, 64], P('groups'), parts along dimension 0
- grad_inner: float32 [128, 64], P('groups'), parts along dimension 0
- grad_last: float32 [128, 1024], P('groups'), parts along dimension 0
The draws below stay inside these ranges and needn't reach their ends.
There are 2 independent parts, one for each index of `groups`. The reference program is written for one: setup_inputs(seed, part) draws one part's arguments, and reference() takes and returns one part's arrays. A program takes and returns all parts, laid end to end along the dimension named above; an argument that names none is the same for every part. Nothing has to cross between parts.
All inputs are finite; a program needn't handle non-finite values.
Results may differ from the reference program's by a relative error of at most 0.0003.
Values may be sent and summed in bfloat16 or wider, within the bound.
A program may use at most 64 MiB of HBM per device.

```python
import math
import jax
import jax.numpy as jnp
from jax import lax

C = 1024
K = 64
E = 5
L = 4096
SEQ = 512
BATCH = 4


def level_of(rng, extent, cuts, least, high):
    loudness = 1.0
    for dim, parts in cuts:
        steps = jax.random.uniform(jax.random.fold_in(jax.random.fold_in(rng, 6), dim), (parts,), jnp.float32, least / len(cuts), high / len(cuts))
        loudness = loudness * jnp.repeat(jnp.exp(steps), extent[dim] // parts).reshape((-1,) + (1,) * (len(extent) - 1 - dim))
    return loudness


def noise(own_key, shape, spread, reach, shards=(), kind=jnp.bfloat16):
    level = level_of(own_key, shape, shards, -0.22, 0.18) if shards else 1.0
    result = jax.random.normal(own_key, shape, jnp.float32) * spread * level
    return jnp.minimum(jnp.maximum(result, -reach), reach).astype(kind)


def setup_inputs(seed: int = 0, part: int = 0) -> dict:
    key_list = jax.random.split(jax.random.key(seed), 8)
    part_splits = jax.random.split(jax.random.fold_in(key_list[7], part), 8)
    values = noise(part_splits[0], (BATCH, SEQ, C), 1.0, 6.0, ((0, 4), (1, 4)))
    grads_out = noise(part_splits[1], (BATCH, SEQ, C), 1.0, 6.0, ((0, 4), (1, 4)))
    w_first = noise(key_list[2], (E, K), E ** -0.5, 2.5, (), jnp.float32)
    sine_freq = jnp.clip(jax.random.uniform(key_list[3], (K,), jnp.float32, 0.5, 2.0), 0.5, 2.0)
    w_inner = noise(key_list[4], (K, K), K ** -0.5, 0.75, (), jnp.float32)
    w_last = noise(key_list[5], (K, C), K ** -0.5, 0.75, (), jnp.float32)
    decay_rates = jnp.clip(jnp.exp(jax.random.uniform(key_list[6], (C,), jnp.float32, math.log(5.999999848427251e-05), math.log(0.03))), 5.999999848427251e-05, 0.03)
    return {"values": values, "grads_out": grads_out, "w_first": w_first, "sine_freq": sine_freq, "w_inner": w_inner, "w_last": w_last, "decay_rates": decay_rates}


HIGHEST_PREC = lax.Precision.HIGHEST

def position_features(offset, row_count, lag_total):
    positions = offset + jnp.arange(row_count, dtype=jnp.int32)
    columns = [positions.astype(jnp.float32) / lag_total]
    for band_idx in (1, 2):
        phase_idx = positions * band_idx % lag_total
        angles = 2.0 * math.pi * phase_idx.astype(jnp.float32) / lag_total
        columns.append(jnp.cos(angles))
        columns.append(jnp.sin(angles))
    return jnp.stack(columns, axis=1)

def filter_outputs(w_first, sine_freq, w_inner, w_last, features):
    pre_first = jnp.dot(features, w_first, precision=HIGHEST_PREC, preferred_element_type=jnp.float32)
    act_first = jnp.sin(sine_freq * pre_first)
    pre_inner = jnp.dot(act_first, w_inner, precision=HIGHEST_PREC, preferred_element_type=jnp.float32)
    act_inner = jnp.sin(sine_freq * pre_inner)
    return jnp.dot(act_inner, w_last, precision=HIGHEST_PREC, preferred_element_type=jnp.float32)

def lag_gradients(values, grads_out):
    length = SEQ + L
    val_spec = jnp.fft.rfft(values.astype(jnp.float32), n=length, axis=1)
    grad_spec = jnp.fft.rfft(grads_out.astype(jnp.float32), n=length, axis=1)
    product = lax.optimization_barrier(jnp.sum(grad_spec * jnp.conj(val_spec), axis=0))
    return jnp.fft.irfft(product, n=length, axis=0)[:L]

def reference(values, grads_out, w_first, sine_freq, w_inner, w_last, decay_rates):
    lagged = lag_gradients(values, grads_out)
    lag_pos = jnp.arange(L, dtype=jnp.float32)
    window = jnp.exp(-lag_pos[:, None] * decay_rates[None, :])
    grad_scale = 1.0 / math.sqrt(BATCH * SEQ * L)
    cotangent = lagged * window * grad_scale
    features = position_features(0, L, L)

    def filter_fn(first_layer, inner_layer, last_layer):
        return filter_outputs(first_layer, sine_freq, inner_layer, last_layer, features)
    raw_filter, pullback = jax.vjp(filter_fn, w_first, w_inner, w_last)
    grad_first, grad_inner, grad_last = pullback(cotangent.astype(raw_filter.dtype))
    return (grad_first, grad_inner, grad_last)
```

```python
import functools
import math

import jax
import jax.numpy as jnp
import ml_dtypes
import numpy as np
from jax import lax
from jax.experimental import pallas as pl
from jax.experimental.pallas import tpu as pltpu
from jax.sharding import PartitionSpec as P

L = 4096


HIGHEST_PREC = lax.Precision.HIGHEST


def shifted(value, axis, steps):
    count = lax.axis_size(axis)
    initial, last = (max(0, -steps), min(count, count - steps))
    return lax.ppermute(value, axis, [(source, source + steps) for source in range(initial, last)])


def position_features(row_count, lag_total):
    positions = jnp.arange(row_count, dtype=jnp.int32)
    columns = [positions.astype(jnp.float32) / lag_total]
    for band_idx in (1, 2):
        phase_idx = positions * band_idx % lag_total
        angles = 2.0 * math.pi * phase_idx.astype(jnp.float32) / lag_total
        columns.append(jnp.cos(angles))
        columns.append(jnp.sin(angles))
    return jnp.stack(columns, axis=1)


def filter_forward(features, w_first, w_inner, sine_freq):
    pre_first = jnp.dot(
        features, w_first, precision=HIGHEST_PREC, preferred_element_type=jnp.float32
    )
    act_first = jnp.sin(sine_freq * pre_first)
    pre_inner = jnp.dot(
        act_first, w_inner, precision=HIGHEST_PREC, preferred_element_type=jnp.float32
    )
    act_inner = jnp.sin(sine_freq * pre_inner)
    return (pre_first, act_first, pre_inner, act_inner)


def filter_back(features, pre_first, act_first, pre_inner, grad_act, w_inner, sine_freq):
    grad_pre = grad_act * sine_freq * jnp.cos(sine_freq * pre_inner)
    grad_inner = jnp.dot(
        act_first.T, grad_pre, precision=HIGHEST_PREC, preferred_element_type=jnp.float32
    )
    grad_act_first = jnp.dot(
        grad_pre, w_inner.T, precision=HIGHEST_PREC, preferred_element_type=jnp.float32
    )
    grad_pre_first = grad_act_first * sine_freq * jnp.cos(sine_freq * pre_first)
    grad_first = jnp.dot(
        features.T, grad_pre_first, precision=HIGHEST_PREC, preferred_element_type=jnp.float32
    )
    return (grad_first, grad_inner)


def spectral_tables(block_len):
    full_len = 2 * block_len
    freq_idx = jnp.arange(block_len, dtype=jnp.int32)
    places = jnp.arange(full_len, dtype=jnp.int32)
    phase_idx = freq_idx[:, None] * places[None, :] % full_len
    angles = math.pi * phase_idx.astype(jnp.float32) / block_len
    back_phase = freq_idx[:, None] * freq_idx[None, :] % full_len
    back_angles = math.pi * back_phase.astype(jnp.float32) / block_len
    weights = jnp.where(freq_idx == 0, 1.0, 2.0).astype(jnp.float32) / full_len
    inv_cos = jnp.cos(back_angles) * weights[None, :]
    inv_sin = jnp.sin(back_angles) * weights[None, :]
    parity = 1.0 - 2.0 * (places % 2).astype(jnp.float32)
    return (jnp.cos(angles), jnp.sin(angles), inv_cos, inv_sin, parity)


def spectrum(cos_part, sin_part, sign_part, signal):
    real_part = jnp.einsum("fn,bnc->bfc", cos_part, signal, precision=HIGHEST_PREC)
    imag_part = -jnp.einsum("fn,bnc->bfc", sin_part, signal, precision=HIGHEST_PREC)
    nyquist = jnp.einsum("n,bnc->bc", sign_part, signal, precision=HIGHEST_PREC)
    return (real_part, imag_part, nyquist)


def lag_block_update(carried, pieces, block_idx, own_spec, shared):
    grad_act, grad_last = carried
    tables, act_inner, w_last, decay_rates, grad_scale = shared
    fwd_cos, fwd_sin, inv_cos, inv_sin, parity = tables
    block_len = inv_cos.shape[0]
    blocks = act_inner.shape[0] // block_len
    own_real, own_imag, own_nyq = own_spec
    in_real, in_imag, in_nyq = spectrum(
        fwd_cos[:, block_len:],
        fwd_sin[:, block_len:],
        parity[block_len:],
        pieces.astype(jnp.float32),
    )
    cross_real = jnp.sum(in_real * own_real + in_imag * own_imag, axis=0)
    cross_imag = jnp.sum(in_imag * own_real - in_real * own_imag, axis=0)
    cross_nyq = jnp.sum(in_nyq * own_nyq, axis=0)
    lagged = jnp.dot(
        inv_cos, cross_real, precision=HIGHEST_PREC, preferred_element_type=jnp.float32
    )
    lagged = lagged - jnp.dot(
        inv_sin, cross_imag, precision=HIGHEST_PREC, preferred_element_type=jnp.float32
    )
    lagged = lagged + (parity[:block_len] / (2 * block_len))[:, None] * cross_nyq[None, :]
    in_range = (block_idx >= 0) & (block_idx < blocks)
    row_start = jnp.clip(block_idx, 0, blocks - 1) * block_len
    lag_pos = (row_start + jnp.arange(block_len, dtype=jnp.int32)).astype(jnp.float32)
    window = jnp.exp(-lag_pos[:, None] * decay_rates[None, :])
    cotangent = jnp.where(in_range, lagged * window * grad_scale, 0.0)
    act_rows = lax.dynamic_slice_in_dim(act_inner, row_start, block_len, 0)
    grad_last = grad_last + jnp.dot(
        act_rows.T, cotangent, precision=HIGHEST_PREC, preferred_element_type=jnp.float32
    )
    current = lax.dynamic_slice_in_dim(grad_act, row_start, block_len, 0)
    update = jnp.dot(
        cotangent, w_last.T, precision=HIGHEST_PREC, preferred_element_type=jnp.float32
    )
    grad_act = lax.dynamic_update_slice_in_dim(grad_act, current + update, row_start, 0)
    return (grad_act, grad_last)


def shards(values, grads_out, w_first, sine_freq, w_inner, w_last, decay_rates):
    block_len = values.shape[1]
    lag_total = L
    tables = spectral_tables(block_len)
    fwd_cos, fwd_sin, inv_cos, inv_sin, parity = tables
    token_count = (
        values.shape[0] * lax.axis_size("dp") * block_len * lax.axis_size("ctx") * lag_total
    )
    grad_scale = 1.0 / math.sqrt(token_count)
    features = position_features(lag_total, lag_total)
    pre_first, act_first, pre_inner, act_inner = filter_forward(
        features, w_first, w_inner, sine_freq
    )
    earlier = shifted(values, "ctx", 1)
    own_pair = jnp.concatenate([earlier, values], axis=1).astype(jnp.float32)
    own_spec = spectrum(fwd_cos, fwd_sin, parity, own_pair)
    shared = (tables, act_inner, w_last, decay_rates, grad_scale)
    carried = (
        jnp.zeros((lag_total, w_last.shape[0]), jnp.float32),
        jnp.zeros(w_last.shape, jnp.float32),
    )
    ctx_index = lax.axis_index("ctx")
    pieces = lax.all_gather(grads_out[None], "ctx", axis=0, tiled=True)

    def one_piece(piece_idx, piece_state):
        return lag_block_update(
            piece_state, pieces[piece_idx], piece_idx - ctx_index, own_spec, shared
        )

    carried = lax.fori_loop(0, pieces.shape[0], one_piece, carried)
    grad_act, grad_last = carried
    grad_act, grad_last = lax.psum((grad_act, grad_last), ("ctx", "dp"))
    grad_first, grad_inner = filter_back(
        features, pre_first, act_first, pre_inner, grad_act, w_inner, sine_freq
    )
    return (grad_first, grad_inner, grad_last)


MESH = pl.DeviceIdType.MESH
FREQ_ROWS = 128


def split_bf16(array):
    high = array.astype(jnp.bfloat16)
    return high, (array - high.astype(jnp.float32)).astype(jnp.bfloat16)


def half_step_tables(total):
    freq = np.arange(total, dtype=np.int64)
    place = np.arange(total, dtype=np.int64)
    phase = ((2 * freq[:, None] + 1) * place[None, :]) % (4 * total)
    angle = np.pi * phase / (2 * total)
    chunks = total // FREQ_ROWS
    cos_part = np.cos(angle).reshape(chunks, FREQ_ROWS, total)
    sin_part = np.sin(angle).reshape(chunks, FREQ_ROWS, total)
    table = np.concatenate([cos_part, sin_part], axis=1).astype(np.float32)
    high = table.astype(ml_dtypes.bfloat16)
    low = (table - high.astype(np.float32)).astype(ml_dtypes.bfloat16)
    flip = lambda part: np.ascontiguousarray(part.transpose(0, 2, 1))
    return high, low, flip(high), flip(low)


def feature_rows(total, rows):
    place = np.arange(total, dtype=np.int64)
    out = np.zeros((rows, total), np.float32)
    out[0] = place / L
    for band in (1, 2):
        angle = 2.0 * np.pi * (place * band % L) / L
        out[2 * band - 1] = np.cos(angle)
        out[2 * band] = np.sin(angle)
    return out


def sin_cos(x):
    turns = jnp.floor(x * np.float32(2.0 / np.pi) + 0.5)
    r = x - turns * np.float32(1.5703125)
    r = r - turns * np.float32(4.837512969970703125e-4)
    r = r - turns * np.float32(7.54978995489188216e-8)
    z = r * r
    s = ((np.float32(-1.9515295891e-4) * z + np.float32(8.3321608736e-3)) * z
         + np.float32(-1.6666654611e-1)) * z * r + r
    c = ((np.float32(2.443315711809948e-5) * z + np.float32(-1.388731625493765e-3)) * z
         + np.float32(4.166664568298827e-2)) * z * z - 0.5 * z + 1.0
    quarter = turns - 4.0 * jnp.floor(turns * 0.25)
    odd = (quarter == 1.0) | (quarter == 3.0)
    sin_flip = jnp.where(quarter >= 2.0, -1.0, 1.0)
    cos_flip = jnp.where((quarter == 1.0) | (quarter == 2.0), -1.0, 1.0)
    return jnp.where(odd, c, s) * sin_flip, jnp.where(odd, s, c) * cos_flip


def dot(a, b, dims=((1,), (0,)), precision=None):
    return lax.dot_general(
        a, b, (dims, ((), ())), precision=precision, preferred_element_type=jnp.float32
    )


def fast_kernel(
    n_ctx, n_dp, scale,
    values, grads, fhi_h, flo_h, ihi_h, ilo_h, w_first, sine_freq, w_inner, w_last, decay, feat,
    out_first, out_inner, out_last,
    tokens, fhi, flo, ihi, ilo, window, lagged, small, partial, quarter, rx, columns, every,
    tab_sem, own_sem, s1, r1, s2, r2, s3, r3, s4, r4,
):
    me = lax.axis_index("ctx")
    md = lax.axis_index("dp")
    block, width = values.shape[1], values.shape[2] // n_ctx
    total = block * n_ctx
    hidden = w_inner.shape[0]
    part = hidden // n_dp

    def ctx_of(k):
        return lax.rem(me + k, n_ctx)

    def dp_of(k):
        return lax.rem(md + k, n_dp)

    tabs = [
        pltpu.make_async_copy(src, dst, tab_sem.at[i])
        for i, (src, dst) in enumerate(
            ((fhi_h, fhi), (flo_h, flo), (ihi_h, ihi), (ilo_h, ilo)))
    ]
    for copy in tabs:
        copy.start()
    my_rows = pl.ds(pl.multiple_of(me * block, block), block)
    my_cols = pl.ds(pl.multiple_of(me * width, width), width)
    own = [
        pltpu.make_async_copy(
            src.at[0, :, my_cols], tokens.at[my_rows, pl.ds(i * width, width)], own_sem.at[i])
        for i, src in enumerate((values, grads))
    ]
    for copy in own:
        copy.start()

    barrier = pltpu.get_barrier_semaphore()
    for k in range(1, n_ctx):
        pl.semaphore_signal(
            barrier, inc=1, device_id={"ctx": ctx_of(k)}, device_id_type=MESH)
    for k in range(1, n_dp):
        pl.semaphore_signal(barrier, inc=1, device_id={"dp": dp_of(k)}, device_id_type=MESH)
    pl.semaphore_wait(barrier, n_ctx + n_dp - 2)

    moves = []
    for k in range(1, n_ctx):
        to = ctx_of(k)
        cols = pl.ds(pl.multiple_of(to * width, width), width)
        for i, src in enumerate((values, grads)):
            move = pltpu.make_async_remote_copy(
                src_ref=src.at[0, :, cols],
                dst_ref=tokens.at[my_rows, pl.ds(i * width, width)],
                send_sem=s1.at[2 * k + i], recv_sem=r1.at[2 * k + i],
                device_id={"ctx": to}, device_id_type=MESH)
            move.start()
            moves.append(move)

    small[...] = jnp.zeros_like(small)
    small[0:hidden, 0:hidden] = w_inner[...]
    small[hidden:hidden + w_first.shape[0], 0:hidden] = w_first[...]
    small[hidden + 8:hidden + 9, 0:hidden] = sine_freq[...]
    turned = small[...].T
    freq = turned[0:hidden, hidden + 8:hidden + 9]
    pre = turned[0:hidden, hidden:hidden + 1] * feat[0:1, :]
    for e in range(1, w_first.shape[0]):
        pre = pre + turned[0:hidden, hidden + e:hidden + e + 1] * feat[e:e + 1, :]
    act_first, slope_first = sin_cos(freq * pre)
    act_inner, slope_inner = sin_cos(
        freq * dot(turned[0:hidden, 0:hidden], act_first, precision=HIGHEST_PREC))
    slope_first = slope_first * freq
    slope_inner = slope_inner * freq
    lag = lax.broadcasted_iota(jnp.int32, (total, width), 0).astype(jnp.float32)
    window[...] = jnp.exp(-lag * decay[:, my_cols]) * np.float32(scale / total)
    for copy in tabs + own:
        copy.wait()
    for move in moves:
        move.wait()

    lagged[...] = jnp.zeros_like(lagged)

    def one_chunk(i, state):
        both = tokens[...]
        spec = dot(fhi[i], both) + dot(flo[i], both)
        v_cos, g_cos = spec[:FREQ_ROWS, :width], spec[:FREQ_ROWS, width:]
        v_sin, g_sin = spec[FREQ_ROWS:, :width], spec[FREQ_ROWS:, width:]
        cross = jnp.concatenate(
            [g_cos * v_cos + g_sin * v_sin, g_sin * v_cos - g_cos * v_sin], axis=0)
        high, low = split_bf16(cross)
        lagged[...] += dot(ihi[i], high) + dot(ihi[i], low) + dot(ilo[i], high)
        return state

    lax.fori_loop(0, total // FREQ_ROWS, one_chunk, 0)
    cot = lagged[...] * window[...]
    partial[:, 0:width] = dot(act_inner, cot, precision=HIGHEST_PREC)
    grad_act = dot(w_last[:, my_cols], cot, ((1,), (1,)), HIGHEST_PREC)
    grad_pre = grad_act * slope_inner
    partial[:, width:width + hidden] = dot(act_first, grad_pre, ((1,), (1,)), HIGHEST_PREC)
    grad_pre_first = dot(w_inner[...], grad_pre, precision=HIGHEST_PREC) * slope_first
    partial[:, width + hidden:width + 2 * hidden] = dot(
        grad_pre_first, feat[...], ((1,), (1,)), HIGHEST_PREC)

    moves = []
    for k in range(1, n_dp):
        to = dp_of(k)
        move = pltpu.make_async_remote_copy(
            src_ref=partial.at[pl.ds(pl.multiple_of(to * part, part), part), :],
            dst_ref=rx.at[k],
            send_sem=s2.at[k], recv_sem=r2.at[k],
            device_id={"dp": to}, device_id_type=MESH)
        move.start()
        moves.append(move)
    summed = partial[pl.ds(pl.multiple_of(md * part, part), part), :]
    for k, move in enumerate(moves):
        move.wait_recv()
        summed = summed + rx[k + 1]
    quarter[...] = summed
    gathers = []
    for k in range(1, n_ctx):
        move = pltpu.make_async_remote_copy(
            src_ref=quarter, dst_ref=every.at[0, k],
            send_sem=s3.at[k], recv_sem=r3.at[k],
            device_id={"ctx": ctx_of(k)}, device_id_type=MESH)
        move.start()
        gathers.append(move)
    every[0, 0] = summed
    spread = []
    for k in range(n_ctx):
        if k:
            gathers[k - 1].wait_recv()
        for a in range(1, n_dp):
            move = pltpu.make_async_remote_copy(
                src_ref=every.at[0, k], dst_ref=every.at[a, k],
                send_sem=s4.at[k * n_dp + a], recv_sem=r4.at[k * n_dp + a],
                device_id={"dp": dp_of(a)}, device_id_type=MESH)
            move.start()
            spread.append((move, a, k))

    def place(a, k):
        rows = pl.ds(pl.multiple_of(lax.rem(md - a + n_dp, n_dp) * part, part), part)
        cols = pl.ds(pl.multiple_of(lax.rem(me - k + n_ctx, n_ctx) * width, width), width)
        out_last[rows, cols] = every[a, k, :, 0:width]
        return rows

    for k in range(n_ctx):
        place(0, k)
    for move, a, k in spread:
        move.wait_recv()
        place(a, k)
    for a in range(n_dp):
        rows = pl.ds(pl.multiple_of(lax.rem(md - a + n_dp, n_dp) * part, part), part)
        tail = jnp.zeros((part, 2 * hidden), jnp.float32)
        for c in range(n_ctx):
            tail = tail + every[a, lax.rem(me - c + n_ctx, n_ctx), :, width:width + 2 * hidden]
        columns[rows, :] = tail
    out_inner[...] = columns[0:hidden, 0:hidden]
    columns_t = columns[...].T
    out_first[...] = columns_t[hidden:hidden + w_first.shape[0], 0:hidden]
    for move in moves + gathers + [item[0] for item in spread]:
        move.wait_send()


def fast_shards(values, grads_out, w_first, sine_freq, w_inner, w_last, decay_rates):
    n_ctx, n_dp = lax.axis_size("ctx"), lax.axis_size("dp")
    block, channels = values.shape[1:]
    total, width = block * n_ctx, channels // n_ctx
    hidden = w_inner.shape[0]
    part = hidden // n_dp
    chunks = total // FREQ_ROWS
    scale = 1.0 / math.sqrt(values.shape[0] * n_dp * total * L)
    tables = half_step_tables(total)
    feat = feature_rows(total, hidden)
    anywhere = pl.BlockSpec(memory_space=pl.ANY)
    near = pl.BlockSpec(memory_space=pltpu.VMEM)
    f32, bf16 = jnp.float32, jnp.bfloat16
    dma = pltpu.SemaphoreType.DMA
    tail = width + 2 * hidden
    return pl.pallas_call(
        functools.partial(fast_kernel, n_ctx, n_dp, scale),
        out_shape=(
            jax.ShapeDtypeStruct(w_first.shape, f32),
            jax.ShapeDtypeStruct(w_inner.shape, f32),
            jax.ShapeDtypeStruct(w_last.shape, f32),
        ),
        in_specs=[anywhere] * 6 + [near] * 6,
        out_specs=(near,) * 3,
        scratch_shapes=[
            pltpu.VMEM((total, 2 * width), bf16),
            pltpu.VMEM(tables[0].shape, bf16),
            pltpu.VMEM(tables[1].shape, bf16),
            pltpu.VMEM(tables[2].shape, bf16),
            pltpu.VMEM(tables[3].shape, bf16),
            pltpu.VMEM((total, width), f32),
            pltpu.VMEM((total, width), f32),
            pltpu.VMEM((2 * hidden, 2 * hidden), f32),
            pltpu.VMEM((hidden, tail), f32),
            pltpu.VMEM((part, tail), f32),
            pltpu.VMEM((n_dp, part, tail), f32),
            pltpu.VMEM((hidden, 2 * hidden), f32),
            pltpu.VMEM((n_dp, n_ctx, part, tail), f32),
            dma((4,)), dma((2,)),
            dma((2 * n_ctx,)), dma((2 * n_ctx,)),
            dma((n_dp,)), dma((n_dp,)),
            dma((n_ctx,)), dma((n_ctx,)),
            dma((n_ctx * n_dp,)), dma((n_ctx * n_dp,)),
        ],
        compiler_params=pltpu.CompilerParams(
            collective_id=0, has_side_effects=True, vmem_limit_bytes=40 * 1024 * 1024),
        name="lag_gradients",
    )(values, grads_out, *tables, w_first, sine_freq[None], w_inner, w_last,
      decay_rates[None], feat)


def fits_fast(mesh, values, w_inner, w_last):
    n_ctx, n_dp = mesh.shape["ctx"], mesh.shape["dp"]
    total, channels, hidden = values.shape[1], values.shape[2], w_inner.shape[0]
    return (
        n_ctx > 1 and n_dp > 1 and total <= min(L, 512) and total % FREQ_ROWS == 0
        and total // n_ctx % 16 == 0 and channels % (n_ctx * 128) == 0
        and hidden == 64 and hidden % (8 * n_dp) == 0
        and values.shape[0] == n_dp * mesh.shape["groups"]
    )


def solution(mesh):
    in_specs = (
        P(("groups", "dp"), "ctx", None),
        P(("groups", "dp"), "ctx", None),
        P(),
        P(),
        P(),
        P(),
        P(),
    )
    out_specs = (P("groups", None), P("groups", None), P("groups", None))

    def whole(values, grads_out, w_first, sine_freq, w_inner, w_last, decay_rates):
        body = fast_shards if fits_fast(mesh, values, w_inner, w_last) else shards
        return jax.shard_map(
            body, mesh=mesh, in_specs=in_specs, out_specs=out_specs, check_vma=False
        )(values, grads_out, w_first, sine_freq, w_inner, w_last, decay_rates)

    return whole
```

```python
import functools
import math

import jax
import jax.numpy as jnp
import ml_dtypes
import numpy as np
from jax import lax
from jax.experimental import pallas as pl
from jax.experimental.pallas import tpu as pltpu
from jax.sharding import PartitionSpec as P

L = 4096


HIGHEST_PREC = lax.Precision.HIGHEST


def shifted(value, axis, steps):
    count = lax.axis_size(axis)
    initial, last = (max(0, -steps), min(count, count - steps))
    return lax.ppermute(value, axis, [(source, source + steps) for source in range(initial, last)])


def position_features(row_count, lag_total):
    positions = jnp.arange(row_count, dtype=jnp.int32)
    columns = [positions.astype(jnp.float32) / lag_total]
    for band_idx in (1, 2):
        phase_idx = positions * band_idx % lag_total
        angles = 2.0 * math.pi * phase_idx.astype(jnp.float32) / lag_total
        columns.append(jnp.cos(angles))
        columns.append(jnp.sin(angles))
    return jnp.stack(columns, axis=1)


def filter_forward(features, w_first, w_inner, sine_freq):
    pre_first = jnp.dot(
        features, w_first, precision=HIGHEST_PREC, preferred_element_type=jnp.float32
    )
    act_first = jnp.sin(sine_freq * pre_first)
    pre_inner = jnp.dot(
        act_first, w_inner, precision=HIGHEST_PREC, preferred_element_type=jnp.float32
    )
    act_inner = jnp.sin(sine_freq * pre_inner)
    return (pre_first, act_first, pre_inner, act_inner)


def filter_back(features, pre_first, act_first, pre_inner, grad_act, w_inner, sine_freq):
    grad_pre = grad_act * sine_freq * jnp.cos(sine_freq * pre_inner)
    grad_inner = jnp.dot(
        act_first.T, grad_pre, precision=HIGHEST_PREC, preferred_element_type=jnp.float32
    )
    grad_act_first = jnp.dot(
        grad_pre, w_inner.T, precision=HIGHEST_PREC, preferred_element_type=jnp.float32
    )
    grad_pre_first = grad_act_first * sine_freq * jnp.cos(sine_freq * pre_first)
    grad_first = jnp.dot(
        features.T, grad_pre_first, precision=HIGHEST_PREC, preferred_element_type=jnp.float32
    )
    return (grad_first, grad_inner)


def spectral_tables(block_len):
    full_len = 2 * block_len
    freq_idx = jnp.arange(block_len, dtype=jnp.int32)
    places = jnp.arange(full_len, dtype=jnp.int32)
    phase_idx = freq_idx[:, None] * places[None, :] % full_len
    angles = math.pi * phase_idx.astype(jnp.float32) / block_len
    back_phase = freq_idx[:, None] * freq_idx[None, :] % full_len
    back_angles = math.pi * back_phase.astype(jnp.float32) / block_len
    weights = jnp.where(freq_idx == 0, 1.0, 2.0).astype(jnp.float32) / full_len
    inv_cos = jnp.cos(back_angles) * weights[None, :]
    inv_sin = jnp.sin(back_angles) * weights[None, :]
    parity = 1.0 - 2.0 * (places % 2).astype(jnp.float32)
    return (jnp.cos(angles), jnp.sin(angles), inv_cos, inv_sin, parity)


def spectrum(cos_part, sin_part, sign_part, signal):
    real_part = jnp.einsum("fn,bnc->bfc", cos_part, signal, precision=HIGHEST_PREC)
    imag_part = -jnp.einsum("fn,bnc->bfc", sin_part, signal, precision=HIGHEST_PREC)
    nyquist = jnp.einsum("n,bnc->bc", sign_part, signal, precision=HIGHEST_PREC)
    return (real_part, imag_part, nyquist)


def lag_block_update(carried, pieces, block_idx, own_spec, shared):
    grad_act, grad_last = carried
    tables, act_inner, w_last, decay_rates, grad_scale = shared
    fwd_cos, fwd_sin, inv_cos, inv_sin, parity = tables
    block_len = inv_cos.shape[0]
    blocks = act_inner.shape[0] // block_len
    own_real, own_imag, own_nyq = own_spec
    in_real, in_imag, in_nyq = spectrum(
        fwd_cos[:, block_len:],
        fwd_sin[:, block_len:],
        parity[block_len:],
        pieces.astype(jnp.float32),
    )
    cross_real = jnp.sum(in_real * own_real + in_imag * own_imag, axis=0)
    cross_imag = jnp.sum(in_imag * own_real - in_real * own_imag, axis=0)
    cross_nyq = jnp.sum(in_nyq * own_nyq, axis=0)
    lagged = jnp.dot(
        inv_cos, cross_real, precision=HIGHEST_PREC, preferred_element_type=jnp.float32
    )
    lagged = lagged - jnp.dot(
        inv_sin, cross_imag, precision=HIGHEST_PREC, preferred_element_type=jnp.float32
    )
    lagged = lagged + (parity[:block_len] / (2 * block_len))[:, None] * cross_nyq[None, :]
    in_range = (block_idx >= 0) & (block_idx < blocks)
    row_start = jnp.clip(block_idx, 0, blocks - 1) * block_len
    lag_pos = (row_start + jnp.arange(block_len, dtype=jnp.int32)).astype(jnp.float32)
    window = jnp.exp(-lag_pos[:, None] * decay_rates[None, :])
    cotangent = jnp.where(in_range, lagged * window * grad_scale, 0.0)
    act_rows = lax.dynamic_slice_in_dim(act_inner, row_start, block_len, 0)
    grad_last = grad_last + jnp.dot(
        act_rows.T, cotangent, precision=HIGHEST_PREC, preferred_element_type=jnp.float32
    )
    current = lax.dynamic_slice_in_dim(grad_act, row_start, block_len, 0)
    update = jnp.dot(
        cotangent, w_last.T, precision=HIGHEST_PREC, preferred_element_type=jnp.float32
    )
    grad_act = lax.dynamic_update_slice_in_dim(grad_act, current + update, row_start, 0)
    return (grad_act, grad_last)


def shards(values, grads_out, w_first, sine_freq, w_inner, w_last, decay_rates):
    block_len = values.shape[1]
    lag_total = L
    tables = spectral_tables(block_len)
    fwd_cos, fwd_sin, inv_cos, inv_sin, parity = tables
    token_count = (
        values.shape[0] * lax.axis_size("dp") * block_len * lax.axis_size("ctx") * lag_total
    )
    grad_scale = 1.0 / math.sqrt(token_count)
    features = position_features(lag_total, lag_total)
    pre_first, act_first, pre_inner, act_inner = filter_forward(
        features, w_first, w_inner, sine_freq
    )
    earlier = shifted(values, "ctx", 1)
    own_pair = jnp.concatenate([earlier, values], axis=1).astype(jnp.float32)
    own_spec = spectrum(fwd_cos, fwd_sin, parity, own_pair)
    shared = (tables, act_inner, w_last, decay_rates, grad_scale)
    carried = (
        jnp.zeros((lag_total, w_last.shape[0]), jnp.float32),
        jnp.zeros(w_last.shape, jnp.float32),
    )
    ctx_index = lax.axis_index("ctx")
    pieces = lax.all_gather(grads_out[None], "ctx", axis=0, tiled=True)

    def one_piece(piece_idx, piece_state):
        return lag_block_update(
            piece_state, pieces[piece_idx], piece_idx - ctx_index, own_spec, shared
        )

    carried = lax.fori_loop(0, pieces.shape[0], one_piece, carried)
    grad_act, grad_last = carried
    grad_act, grad_last = lax.psum((grad_act, grad_last), ("ctx", "dp"))
    grad_first, grad_inner = filter_back(
        features, pre_first, act_first, pre_inner, grad_act, w_inner, sine_freq
    )
    return (grad_first, grad_inner, grad_last)


MESH = pl.DeviceIdType.MESH
FREQ_ROWS = 128
VMEM_BYTES = 60 * 1024 * 1024


def split_bf16(array):
    high = array.astype(jnp.bfloat16)
    return high, (array - high.astype(jnp.float32)).astype(jnp.bfloat16)


def half_step_tables(total):
    freq = np.arange(total, dtype=np.int64)
    place = np.arange(total, dtype=np.int64)
    phase = ((2 * freq[:, None] + 1) * place[None, :]) % (4 * total)
    angle = np.pi * phase / (2 * total)
    chunks = total // FREQ_ROWS
    cos_part = np.cos(angle).reshape(chunks, FREQ_ROWS, total)
    sin_part = np.sin(angle).reshape(chunks, FREQ_ROWS, total)
    table = np.concatenate([cos_part, sin_part], axis=1).astype(np.float32)
    high = table.astype(ml_dtypes.bfloat16)
    low = (table - high.astype(np.float32)).astype(ml_dtypes.bfloat16)
    flip = lambda part: np.ascontiguousarray(part.transpose(0, 2, 1))
    return high, low, flip(high), flip(low)


def feature_rows(total, rows):
    place = np.arange(total, dtype=np.int64)
    out = np.zeros((rows, total), np.float32)
    out[0] = place / L
    for band in (1, 2):
        angle = 2.0 * np.pi * (place * band % L) / L
        out[2 * band - 1] = np.cos(angle)
        out[2 * band] = np.sin(angle)
    return out


def sin_cos(x):
    turns = jnp.floor(x * np.float32(2.0 / np.pi) + 0.5)
    r = x - turns * np.float32(1.5703125)
    r = r - turns * np.float32(4.837512969970703125e-4)
    r = r - turns * np.float32(7.54978995489188216e-8)
    z = r * r
    s = ((np.float32(-1.9515295891e-4) * z + np.float32(8.3321608736e-3)) * z
         + np.float32(-1.6666654611e-1)) * z * r + r
    c = ((np.float32(2.443315711809948e-5) * z + np.float32(-1.388731625493765e-3)) * z
         + np.float32(4.166664568298827e-2)) * z * z - 0.5 * z + 1.0
    quarter = turns - 4.0 * jnp.floor(turns * 0.25)
    odd = (quarter == 1.0) | (quarter == 3.0)
    sin_flip = jnp.where(quarter >= 2.0, -1.0, 1.0)
    cos_flip = jnp.where((quarter == 1.0) | (quarter == 2.0), -1.0, 1.0)
    return jnp.where(odd, c, s) * sin_flip, jnp.where(odd, s, c) * cos_flip


def dot(a, b, dims=((1,), (0,)), precision=None):
    return lax.dot_general(
        a, b, (dims, ((), ())), precision=precision, preferred_element_type=jnp.float32
    )


def dot_parts(a, b, dims=((1,), (0,))):
    rows = a[0].shape[0]
    first = dot(jnp.concatenate(a, axis=0), b[0], dims)
    return first[:rows] + first[rows:] + dot(a[0], b[1], dims)


def fast_kernel(
    n_ctx, n_dp, scale,
    values, grads, fhi_h, flo_h, ihi_h, ilo_h,
    w_first_h, sine_freq_h, w_inner_h, w_last_h, decay_h, feat_h,
    out_first, out_inner, out_last,
    w_first, sine_freq, w_inner, w_last, decay, feat,
    tokens, fhi, flo, ihi, ilo, window, small, partial, quarter, rx, columns, every,
    tab_sem, own_sem, s1, r1, s2, r2, s3, r3, s4, r4,
):
    me = lax.axis_index("ctx")
    md = lax.axis_index("dp")
    block, width = values.shape[1], values.shape[2] // n_ctx
    total = block * n_ctx
    hidden = w_inner.shape[0]
    part = hidden // n_dp

    def ctx_of(k):
        return lax.rem(me + k, n_ctx)

    def dp_of(k):
        return lax.rem(md + k, n_dp)

    barrier = pltpu.get_barrier_semaphore()
    for k in range(1, n_ctx):
        pl.semaphore_signal(
            barrier, inc=1, device_id={"ctx": ctx_of(k)}, device_id_type=MESH)
    for k in range(1, n_dp):
        pl.semaphore_signal(barrier, inc=1, device_id={"dp": dp_of(k)}, device_id_type=MESH)
    my_rows = pl.ds(pl.multiple_of(me * block, block), block)
    my_cols = pl.ds(pl.multiple_of(me * width, width), width)
    pairs = (
        (w_first_h, w_first), (sine_freq_h, sine_freq), (w_inner_h, w_inner),
        (decay_h.at[:, my_cols], decay), (feat_h, feat), (w_last_h.at[:, my_cols], w_last),
        (fhi_h, fhi), (flo_h, flo), (ihi_h, ihi), (ilo_h, ilo))
    loads = [
        pltpu.make_async_copy(src, dst, tab_sem.at[i]) for i, (src, dst) in enumerate(pairs)]
    for copy in loads:
        copy.start()
    params, tabs = loads[:6], loads[6:]
    own = [
        pltpu.make_async_copy(
            src.at[0, :, my_cols], tokens.at[my_rows, pl.ds(i * width, width)], own_sem.at[i])
        for i, src in enumerate((values, grads))
    ]
    for copy in own:
        copy.start()

    pl.semaphore_wait(barrier, n_ctx + n_dp - 2)

    moves = []
    for k in range(1, n_ctx):
        to = ctx_of(k)
        cols = pl.ds(pl.multiple_of(to * width, width), width)
        for i, src in enumerate((values, grads)):
            move = pltpu.make_async_remote_copy(
                src_ref=src.at[0, :, cols],
                dst_ref=tokens.at[my_rows, pl.ds(i * width, width)],
                send_sem=s1.at[2 * k + i], recv_sem=r1.at[2 * k + i],
                device_id={"ctx": to}, device_id_type=MESH)
            move.start()
            moves.append(move)

    for copy in params:
        copy.wait()
    small[...] = jnp.zeros_like(small)
    small[0:hidden, 0:hidden] = w_inner[...]
    small[hidden:hidden + w_first.shape[0], 0:hidden] = w_first[...]
    small[hidden + 8:hidden + 9, 0:hidden] = sine_freq[...]
    turned = small[...].T
    freq = turned[0:hidden, hidden + 8:hidden + 9]
    pre = turned[0:hidden, hidden:hidden + 1] * feat[0:1, :]
    for e in range(1, w_first.shape[0]):
        pre = pre + turned[0:hidden, hidden + e:hidden + e + 1] * feat[e:e + 1, :]
    act_first, slope_first = sin_cos(freq * pre)
    act_inner, slope_inner = sin_cos(
        freq * dot(turned[0:hidden, 0:hidden], act_first, precision=HIGHEST_PREC))
    act_inner_parts, act_first_parts = split_bf16(act_inner), split_bf16(act_first)
    w_last_parts, w_inner_parts = split_bf16(w_last[...]), split_bf16(w_inner[...])
    feat_parts = split_bf16(feat[...])
    slope_first = slope_first * freq
    slope_inner = slope_inner * freq
    lag = lax.broadcasted_iota(jnp.int32, (total, width), 0).astype(jnp.float32)
    window[...] = jnp.exp(-lag * decay[...]) * np.float32(scale / total)
    for copy in tabs + own:
        copy.wait()
    for move in moves:
        move.wait()

    both = tokens[...]
    lagged = None
    for i in range(total // FREQ_ROWS):
        spec = dot(fhi[i], both) + dot(flo[i], both)
        v_cos, g_cos = spec[:FREQ_ROWS, :width], spec[:FREQ_ROWS, width:]
        v_sin, g_sin = spec[FREQ_ROWS:, :width], spec[FREQ_ROWS:, width:]
        cross = jnp.concatenate(
            [g_cos * v_cos + g_sin * v_sin, g_sin * v_cos - g_cos * v_sin], axis=0)
        high, low = split_bf16(cross)
        update = dot(ihi[i], high) + dot(ihi[i], low) + dot(ilo[i], high)
        lagged = update if lagged is None else lagged + update
    cot = split_bf16(lagged * window[...])
    across = ((1,), (1,))
    partial[:, 0:width] = dot_parts(act_inner_parts, cot)
    grad_pre = dot_parts(w_last_parts, cot, across) * slope_inner
    grad_parts = split_bf16(grad_pre)
    partial[:, width:width + hidden] = dot_parts(act_first_parts, grad_parts, across)
    grad_pre_first = dot_parts(w_inner_parts, grad_parts) * slope_first
    partial[:, width + hidden:width + 2 * hidden] = dot_parts(
        split_bf16(grad_pre_first), feat_parts, across)

    moves = []
    for k in range(1, n_dp):
        to = dp_of(k)
        move = pltpu.make_async_remote_copy(
            src_ref=partial.at[pl.ds(pl.multiple_of(to * part, part), part), :],
            dst_ref=rx.at[k],
            send_sem=s2.at[k], recv_sem=r2.at[k],
            device_id={"dp": to}, device_id_type=MESH)
        move.start()
        moves.append(move)
    summed = partial[pl.ds(pl.multiple_of(md * part, part), part), :]
    for k, move in enumerate(moves):
        move.wait_recv()
        summed = summed + rx[k + 1]
    quarter[...] = summed
    gathers = []
    for k in range(1, n_ctx):
        move = pltpu.make_async_remote_copy(
            src_ref=quarter, dst_ref=every.at[0, k],
            send_sem=s3.at[k], recv_sem=r3.at[k],
            device_id={"ctx": ctx_of(k)}, device_id_type=MESH)
        move.start()
        gathers.append(move)
    every[0, 0] = summed
    spread = []
    for k in range(n_ctx):
        if k:
            gathers[k - 1].wait_recv()
        for a in range(1, n_dp):
            move = pltpu.make_async_remote_copy(
                src_ref=every.at[0, k], dst_ref=every.at[a, k],
                send_sem=s4.at[k * n_dp + a], recv_sem=r4.at[k * n_dp + a],
                device_id={"dp": dp_of(a)}, device_id_type=MESH)
            move.start()
            spread.append((move, a, k))

    def place(a, k):
        rows = pl.ds(pl.multiple_of(lax.rem(md - a + n_dp, n_dp) * part, part), part)
        cols = pl.ds(pl.multiple_of(lax.rem(me - k + n_ctx, n_ctx) * width, width), width)
        out_last[rows, cols] = every[a, k, :, 0:width]
        return rows

    for k in range(n_ctx):
        place(0, k)
    for move, a, k in spread:
        move.wait_recv()
        place(a, k)
    for a in range(n_dp):
        rows = pl.ds(pl.multiple_of(lax.rem(md - a + n_dp, n_dp) * part, part), part)
        tail = jnp.zeros((part, 2 * hidden), jnp.float32)
        for c in range(n_ctx):
            tail = tail + every[a, lax.rem(me - c + n_ctx, n_ctx), :, width:width + 2 * hidden]
        columns[rows, :] = tail
    out_inner[...] = columns[0:hidden, 0:hidden]
    columns_t = columns[...].T
    out_first[...] = columns_t[hidden:hidden + w_first.shape[0], 0:hidden]
    for move in moves + gathers + [item[0] for item in spread]:
        move.wait_send()


def fast_shards(values, grads_out, w_first, sine_freq, w_inner, w_last, decay_rates):
    n_ctx, n_dp = lax.axis_size("ctx"), lax.axis_size("dp")
    block, channels = values.shape[1:]
    total, width = block * n_ctx, channels // n_ctx
    hidden = w_inner.shape[0]
    part = hidden // n_dp
    chunks = total // FREQ_ROWS
    scale = 1.0 / math.sqrt(values.shape[0] * n_dp * total * L)
    tables = half_step_tables(total)
    feat = feature_rows(total, hidden)
    anywhere = pl.BlockSpec(memory_space=pl.ANY)
    near = pl.BlockSpec(memory_space=pltpu.VMEM)
    f32, bf16 = jnp.float32, jnp.bfloat16
    dma = pltpu.SemaphoreType.DMA
    tail = width + 2 * hidden
    return pl.pallas_call(
        functools.partial(fast_kernel, n_ctx, n_dp, scale),
        out_shape=(
            jax.ShapeDtypeStruct(w_first.shape, f32),
            jax.ShapeDtypeStruct(w_inner.shape, f32),
            jax.ShapeDtypeStruct(w_last.shape, f32),
        ),
        in_specs=[anywhere] * 12,
        out_specs=(near,) * 3,
        scratch_shapes=[
            pltpu.VMEM(w_first.shape, f32),
            pltpu.VMEM((1, hidden), f32),
            pltpu.VMEM(w_inner.shape, f32),
            pltpu.VMEM((hidden, width), f32),
            pltpu.VMEM((1, width), f32),
            pltpu.VMEM(feat.shape, f32),
            pltpu.VMEM((total, 2 * width), bf16),
            pltpu.VMEM(tables[0].shape, bf16),
            pltpu.VMEM(tables[1].shape, bf16),
            pltpu.VMEM(tables[2].shape, bf16),
            pltpu.VMEM(tables[3].shape, bf16),
            pltpu.VMEM((total, width), f32),
            pltpu.VMEM((2 * hidden, 2 * hidden), f32),
            pltpu.VMEM((hidden, tail), f32),
            pltpu.VMEM((part, tail), f32),
            pltpu.VMEM((n_dp, part, tail), f32),
            pltpu.VMEM((hidden, 2 * hidden), f32),
            pltpu.VMEM((n_dp, n_ctx, part, tail), f32),
            dma((10,)), dma((2,)),
            dma((2 * n_ctx,)), dma((2 * n_ctx,)),
            dma((n_dp,)), dma((n_dp,)),
            dma((n_ctx,)), dma((n_ctx,)),
            dma((n_ctx * n_dp,)), dma((n_ctx * n_dp,)),
        ],
        compiler_params=pltpu.CompilerParams(
            collective_id=0, has_side_effects=True, vmem_limit_bytes=VMEM_BYTES),
        name="lag_gradients",
    )(values, grads_out, *tables, w_first, sine_freq[None], w_inner, w_last,
      decay_rates[None], feat)


def fits_fast(mesh, values, w_inner, w_last):
    n_ctx, n_dp = mesh.shape["ctx"], mesh.shape["dp"]
    total, channels, hidden = values.shape[1], values.shape[2], w_inner.shape[0]
    return (
        n_ctx > 1 and n_dp > 1 and total <= min(L, 512) and total % FREQ_ROWS == 0
        and total // n_ctx % 16 == 0 and channels % (n_ctx * 128) == 0
        and hidden == 64 and hidden % (8 * n_dp) == 0
        and values.shape[0] == n_dp * mesh.shape["groups"]
    )


def solution(mesh):
    in_specs = (
        P(("groups", "dp"), "ctx", None),
        P(("groups", "dp"), "ctx", None),
        P(),
        P(),
        P(),
        P(),
        P(),
    )
    out_specs = (P("groups", None), P("groups", None), P("groups", None))

    def whole(values, grads_out, w_first, sine_freq, w_inner, w_last, decay_rates):
        body = fast_shards if fits_fast(mesh, values, w_inner, w_last) else shards
        return jax.shard_map(
            body, mesh=mesh, in_specs=in_specs, out_specs=out_specs, check_vma=False
        )(values, grads_out, w_first, sine_freq, w_inner, w_last, decay_rates)

    return whole
```

```python
import functools
import math

import jax
import jax.numpy as jnp
import ml_dtypes
import numpy as np
from jax import lax
from jax.experimental import pallas as pl
from jax.experimental.pallas import tpu as pltpu
from jax.sharding import PartitionSpec as P

L = 4096


HIGHEST_PREC = lax.Precision.HIGHEST


def shifted(value, axis, steps):
    count = lax.axis_size(axis)
    initial, last = (max(0, -steps), min(count, count - steps))
    return lax.ppermute(value, axis, [(source, source + steps) for source in range(initial, last)])


def position_features(row_count, lag_total):
    positions = jnp.arange(row_count, dtype=jnp.int32)
    columns = [positions.astype(jnp.float32) / lag_total]
    for band_idx in (1, 2):
        phase_idx = positions * band_idx % lag_total
        angles = 2.0 * math.pi * phase_idx.astype(jnp.float32) / lag_total
        columns.append(jnp.cos(angles))
        columns.append(jnp.sin(angles))
    return jnp.stack(columns, axis=1)


def filter_forward(features, w_first, w_inner, sine_freq):
    pre_first = jnp.dot(
        features, w_first, precision=HIGHEST_PREC, preferred_element_type=jnp.float32
    )
    act_first = jnp.sin(sine_freq * pre_first)
    pre_inner = jnp.dot(
        act_first, w_inner, precision=HIGHEST_PREC, preferred_element_type=jnp.float32
    )
    act_inner = jnp.sin(sine_freq * pre_inner)
    return (pre_first, act_first, pre_inner, act_inner)


def filter_back(features, pre_first, act_first, pre_inner, grad_act, w_inner, sine_freq):
    grad_pre = grad_act * sine_freq * jnp.cos(sine_freq * pre_inner)
    grad_inner = jnp.dot(
        act_first.T, grad_pre, precision=HIGHEST_PREC, preferred_element_type=jnp.float32
    )
    grad_act_first = jnp.dot(
        grad_pre, w_inner.T, precision=HIGHEST_PREC, preferred_element_type=jnp.float32
    )
    grad_pre_first = grad_act_first * sine_freq * jnp.cos(sine_freq * pre_first)
    grad_first = jnp.dot(
        features.T, grad_pre_first, precision=HIGHEST_PREC, preferred_element_type=jnp.float32
    )
    return (grad_first, grad_inner)


def spectral_tables(block_len):
    full_len = 2 * block_len
    freq_idx = jnp.arange(block_len, dtype=jnp.int32)
    places = jnp.arange(full_len, dtype=jnp.int32)
    phase_idx = freq_idx[:, None] * places[None, :] % full_len
    angles = math.pi * phase_idx.astype(jnp.float32) / block_len
    back_phase = freq_idx[:, None] * freq_idx[None, :] % full_len
    back_angles = math.pi * back_phase.astype(jnp.float32) / block_len
    weights = jnp.where(freq_idx == 0, 1.0, 2.0).astype(jnp.float32) / full_len
    inv_cos = jnp.cos(back_angles) * weights[None, :]
    inv_sin = jnp.sin(back_angles) * weights[None, :]
    parity = 1.0 - 2.0 * (places % 2).astype(jnp.float32)
    return (jnp.cos(angles), jnp.sin(angles), inv_cos, inv_sin, parity)


def spectrum(cos_part, sin_part, sign_part, signal):
    real_part = jnp.einsum("fn,bnc->bfc", cos_part, signal, precision=HIGHEST_PREC)
    imag_part = -jnp.einsum("fn,bnc->bfc", sin_part, signal, precision=HIGHEST_PREC)
    nyquist = jnp.einsum("n,bnc->bc", sign_part, signal, precision=HIGHEST_PREC)
    return (real_part, imag_part, nyquist)


def lag_block_update(carried, pieces, block_idx, own_spec, shared):
    grad_act, grad_last = carried
    tables, act_inner, w_last, decay_rates, grad_scale = shared
    fwd_cos, fwd_sin, inv_cos, inv_sin, parity = tables
    block_len = inv_cos.shape[0]
    blocks = act_inner.shape[0] // block_len
    own_real, own_imag, own_nyq = own_spec
    in_real, in_imag, in_nyq = spectrum(
        fwd_cos[:, block_len:],
        fwd_sin[:, block_len:],
        parity[block_len:],
        pieces.astype(jnp.float32),
    )
    cross_real = jnp.sum(in_real * own_real + in_imag * own_imag, axis=0)
    cross_imag = jnp.sum(in_imag * own_real - in_real * own_imag, axis=0)
    cross_nyq = jnp.sum(in_nyq * own_nyq, axis=0)
    lagged = jnp.dot(
        inv_cos, cross_real, precision=HIGHEST_PREC, preferred_element_type=jnp.float32
    )
    lagged = lagged - jnp.dot(
        inv_sin, cross_imag, precision=HIGHEST_PREC, preferred_element_type=jnp.float32
    )
    lagged = lagged + (parity[:block_len] / (2 * block_len))[:, None] * cross_nyq[None, :]
    in_range = (block_idx >= 0) & (block_idx < blocks)
    row_start = jnp.clip(block_idx, 0, blocks - 1) * block_len
    lag_pos = (row_start + jnp.arange(block_len, dtype=jnp.int32)).astype(jnp.float32)
    window = jnp.exp(-lag_pos[:, None] * decay_rates[None, :])
    cotangent = jnp.where(in_range, lagged * window * grad_scale, 0.0)
    act_rows = lax.dynamic_slice_in_dim(act_inner, row_start, block_len, 0)
    grad_last = grad_last + jnp.dot(
        act_rows.T, cotangent, precision=HIGHEST_PREC, preferred_element_type=jnp.float32
    )
    current = lax.dynamic_slice_in_dim(grad_act, row_start, block_len, 0)
    update = jnp.dot(
        cotangent, w_last.T, precision=HIGHEST_PREC, preferred_element_type=jnp.float32
    )
    grad_act = lax.dynamic_update_slice_in_dim(grad_act, current + update, row_start, 0)
    return (grad_act, grad_last)


def shards(values, grads_out, w_first, sine_freq, w_inner, w_last, decay_rates):
    block_len = values.shape[1]
    lag_total = L
    tables = spectral_tables(block_len)
    fwd_cos, fwd_sin, inv_cos, inv_sin, parity = tables
    token_count = (
        values.shape[0] * lax.axis_size("dp") * block_len * lax.axis_size("ctx") * lag_total
    )
    grad_scale = 1.0 / math.sqrt(token_count)
    features = position_features(lag_total, lag_total)
    pre_first, act_first, pre_inner, act_inner = filter_forward(
        features, w_first, w_inner, sine_freq
    )
    earlier = shifted(values, "ctx", 1)
    own_pair = jnp.concatenate([earlier, values], axis=1).astype(jnp.float32)
    own_spec = spectrum(fwd_cos, fwd_sin, parity, own_pair)
    shared = (tables, act_inner, w_last, decay_rates, grad_scale)
    carried = (
        jnp.zeros((lag_total, w_last.shape[0]), jnp.float32),
        jnp.zeros(w_last.shape, jnp.float32),
    )
    ctx_index = lax.axis_index("ctx")
    pieces = lax.all_gather(grads_out[None], "ctx", axis=0, tiled=True)

    def one_piece(piece_idx, piece_state):
        return lag_block_update(
            piece_state, pieces[piece_idx], piece_idx - ctx_index, own_spec, shared
        )

    carried = lax.fori_loop(0, pieces.shape[0], one_piece, carried)
    grad_act, grad_last = carried
    grad_act, grad_last = lax.psum((grad_act, grad_last), ("ctx", "dp"))
    grad_first, grad_inner = filter_back(
        features, pre_first, act_first, pre_inner, grad_act, w_inner, sine_freq
    )
    return (grad_first, grad_inner, grad_last)


MESH = pl.DeviceIdType.MESH
FREQ_ROWS = 128
VMEM_BYTES = 60 * 1024 * 1024


def split_bf16(array):
    high = array.astype(jnp.bfloat16)
    return high, (array - high.astype(jnp.float32)).astype(jnp.bfloat16)


def half_step_tables(total):
    freq = np.arange(total, dtype=np.int64)
    place = np.arange(total, dtype=np.int64)
    phase = ((2 * freq[:, None] + 1) * place[None, :]) % (4 * total)
    angle = np.pi * phase / (2 * total)
    chunks = total // FREQ_ROWS
    cos_part = np.cos(angle).reshape(chunks, FREQ_ROWS, total)
    sin_part = np.sin(angle).reshape(chunks, FREQ_ROWS, total)
    table = np.concatenate([cos_part, sin_part], axis=1).astype(np.float32)
    high = table.astype(ml_dtypes.bfloat16)
    low = (table - high.astype(np.float32)).astype(ml_dtypes.bfloat16)
    flip = lambda part: np.ascontiguousarray(part.transpose(0, 2, 1))
    return high, low, flip(high), flip(low)


def feature_rows(total, rows):
    place = np.arange(total, dtype=np.int64)
    out = np.zeros((rows, total), np.float32)
    out[0] = place / L
    for band in (1, 2):
        angle = 2.0 * np.pi * (place * band % L) / L
        out[2 * band - 1] = np.cos(angle)
        out[2 * band] = np.sin(angle)
    return out


def sin_cos(x):
    turns = jnp.floor(x * np.float32(2.0 / np.pi) + 0.5)
    r = x - turns * np.float32(1.5703125)
    r = r - turns * np.float32(4.837512969970703125e-4)
    r = r - turns * np.float32(7.54978995489188216e-8)
    z = r * r
    s = ((np.float32(-1.9515295891e-4) * z + np.float32(8.3321608736e-3)) * z
         + np.float32(-1.6666654611e-1)) * z * r + r
    c = ((np.float32(2.443315711809948e-5) * z + np.float32(-1.388731625493765e-3)) * z
         + np.float32(4.166664568298827e-2)) * z * z - 0.5 * z + 1.0
    quarter = turns - 4.0 * jnp.floor(turns * 0.25)
    odd = (quarter == 1.0) | (quarter == 3.0)
    sin_flip = jnp.where(quarter >= 2.0, -1.0, 1.0)
    cos_flip = jnp.where((quarter == 1.0) | (quarter == 2.0), -1.0, 1.0)
    return jnp.where(odd, c, s) * sin_flip, jnp.where(odd, s, c) * cos_flip


def dot(a, b, dims=((1,), (0,)), precision=None):
    return lax.dot_general(
        a, b, (dims, ((), ())), precision=precision, preferred_element_type=jnp.float32
    )


def dot_parts(a, b, dims=((1,), (0,))):
    rows = a[0].shape[0]
    first = dot(jnp.concatenate(a, axis=0), b[0], dims)
    return first[:rows] + first[rows:] + dot(a[0], b[1], dims)


def fast_kernel(
    n_ctx, n_dp, scale,
    values, grads, fhi_h, flo_h, ihi_h, ilo_h,
    w_first_h, sine_freq_h, w_inner_h, w_last_h, decay_h, feat_h,
    out_first, out_inner, out_last,
    w_first, sine_freq, w_inner, w_last, decay, feat,
    tokens, fhi, flo, ihi, ilo, window, small, partial, rx, columns, landed, every, tails, spectra,
    tab_sem, own_sem, s1, r1, s2, r2, s3, r3, s4, r4,
):
    me = lax.axis_index("ctx")
    md = lax.axis_index("dp")
    block, width = values.shape[1], values.shape[2] // n_ctx
    total = block * n_ctx
    hidden = w_inner.shape[0]
    part = hidden // n_dp

    def ctx_of(k):
        return lax.rem(me + k, n_ctx)

    def dp_of(k):
        return lax.rem(md + k, n_dp)

    barrier = pltpu.get_barrier_semaphore()
    for k in range(1, n_ctx):
        pl.semaphore_signal(
            barrier, inc=1, device_id={"ctx": ctx_of(k)}, device_id_type=MESH)
    for k in range(1, n_dp):
        pl.semaphore_signal(barrier, inc=1, device_id={"dp": dp_of(k)}, device_id_type=MESH)
    my_rows = pl.ds(pl.multiple_of(me * block, block), block)
    my_cols = pl.ds(pl.multiple_of(me * width, width), width)
    pairs = (
        (w_first_h, w_first), (sine_freq_h, sine_freq), (w_inner_h, w_inner),
        (decay_h.at[:, my_cols], decay), (feat_h, feat), (w_last_h.at[:, my_cols], w_last),
        (fhi_h, fhi), (flo_h, flo), (ihi_h, ihi), (ilo_h, ilo))
    loads = [
        pltpu.make_async_copy(src, dst, tab_sem.at[i]) for i, (src, dst) in enumerate(pairs)]
    for copy in loads:
        copy.start()
    params, tabs = loads[:6], loads[6:]
    own = [
        pltpu.make_async_copy(
            src.at[0, :, my_cols], tokens.at[my_rows, pl.ds(i * width, width)], own_sem.at[i])
        for i, src in enumerate((values, grads))
    ]
    for copy in own:
        copy.start()

    pl.semaphore_wait(barrier, n_ctx + n_dp - 2)

    moves = []
    for i, src in enumerate((values, grads)):
        for k in (2, 1, 3) if n_ctx == 4 else range(1, n_ctx):
            to = ctx_of(k)
            cols = pl.ds(pl.multiple_of(to * width, width), width)
            move = pltpu.make_async_remote_copy(
                src_ref=src.at[0, :, cols],
                dst_ref=tokens.at[my_rows, pl.ds(i * width, width)],
                send_sem=s1.at[2 * k + i], recv_sem=r1.at[2 * k + i],
                device_id={"ctx": to}, device_id_type=MESH)
            move.start()
            moves.append(move)

    for copy in params:
        copy.wait()
    small[...] = jnp.zeros_like(small)
    small[0:hidden, 0:hidden] = w_inner[...]
    small[hidden:hidden + w_first.shape[0], 0:hidden] = w_first[...]
    small[hidden + 8:hidden + 9, 0:hidden] = sine_freq[...]
    turned = small[...].T
    freq = turned[0:hidden, hidden + 8:hidden + 9]
    pre = turned[0:hidden, hidden:hidden + 1] * feat[0:1, :]
    for e in range(1, w_first.shape[0]):
        pre = pre + turned[0:hidden, hidden + e:hidden + e + 1] * feat[e:e + 1, :]
    act_first, slope_first = sin_cos(freq * pre)
    act_inner, slope_inner = sin_cos(
        freq * dot(turned[0:hidden, 0:hidden], act_first, precision=HIGHEST_PREC))
    act_inner_parts, act_first_parts = split_bf16(act_inner), split_bf16(act_first)
    w_last_parts, w_inner_parts = split_bf16(w_last[...]), split_bf16(w_inner[...])
    feat_parts = split_bf16(feat[...])
    slope_first = slope_first * freq
    slope_inner = slope_inner * freq
    lag = lax.broadcasted_iota(jnp.int32, (total, width), 0).astype(jnp.float32)
    window[...] = jnp.exp(-lag * decay[...]) * np.float32(scale / total)
    for copy in tabs + own:
        copy.wait()
    sent, moves = moves, None
    for move in sent[:n_ctx - 1]:
        move.wait_recv()
    held = tokens[:, :width]
    for i in range(total // FREQ_ROWS):
        spectra[i] = dot(fhi[i], held) + dot(flo[i], held)
    for move in sent[n_ctx - 1:]:
        move.wait_recv()

    held = tokens[:, width:]
    lagged = None
    for i in range(total // FREQ_ROWS):
        spec = dot(fhi[i], held) + dot(flo[i], held)
        v_cos, v_sin = spectra[i, :FREQ_ROWS], spectra[i, FREQ_ROWS:]
        g_cos, g_sin = spec[:FREQ_ROWS], spec[FREQ_ROWS:]
        cross = jnp.concatenate(
            [g_cos * v_cos + g_sin * v_sin, g_sin * v_cos - g_cos * v_sin], axis=0)
        high, low = split_bf16(cross)
        update = dot(ihi[i], high) + dot(ihi[i], low) + dot(ilo[i], high)
        lagged = update if lagged is None else lagged + update
    cot = split_bf16(lagged * window[...])
    across = ((1,), (1,))
    partial[:, 0:width] = dot_parts(act_inner_parts, cot)
    grad_pre = dot_parts(w_last_parts, cot, across) * slope_inner
    grad_parts = split_bf16(grad_pre)
    partial[:, width:width + hidden] = dot_parts(act_first_parts, grad_parts, across)
    grad_pre_first = dot_parts(w_inner_parts, grad_parts) * slope_first
    partial[:, width + hidden:width + 2 * hidden] = dot_parts(
        split_bf16(grad_pre_first), feat_parts, across)

    moves = []
    for k in range(1, n_dp):
        to = dp_of(k)
        move = pltpu.make_async_remote_copy(
            src_ref=partial.at[pl.ds(pl.multiple_of(to * part, part), part), :],
            dst_ref=rx.at[k],
            send_sem=s2.at[k], recv_sem=r2.at[k],
            device_id={"dp": to}, device_id_type=MESH)
        move.start()
        moves.append(move)
    summed = partial[pl.ds(pl.multiple_of(md * part, part), part), :]
    for k, move in enumerate(moves):
        move.wait_recv()
        summed = summed + rx[k + 1]
    landed[0] = summed
    gathers = []
    for k in range(1, n_ctx):
        move = pltpu.make_async_remote_copy(
            src_ref=landed.at[0], dst_ref=landed.at[k],
            send_sem=s3.at[k], recv_sem=r3.at[k],
            device_id={"ctx": ctx_of(k)}, device_id_type=MESH)
        move.start()
        gathers.append(move)

    mate = md + 1 - 2 * lax.rem(md, 2)
    far = lax.rem(md + 2, 4)
    rows_of = [
        pl.ds(pl.multiple_of(q * part, part), part)
        for q in (md, mate, far, lax.rem(mate + 2, 4))]

    def pass_on(src, dst, k, a):
        move = pltpu.make_async_remote_copy(
            src_ref=src, dst_ref=dst, send_sem=s4.at[4 * k + a], recv_sem=r4.at[4 * k + a],
            device_id={"dp": far if a == 2 else mate}, device_id_type=MESH)
        move.start()
        return move

    def place(block, a, k):
        cols = pl.ds(pl.multiple_of(lax.rem(me - k + n_ctx, n_ctx) * width, width), width)
        out_last[rows_of[a], cols] = block

    spread = [[None] * 4 for _ in range(n_ctx + 1)]
    for k in range(n_ctx):
        if k:
            gathers[k - 1].wait_recv()
        for a in (2, 1):
            spread[k][a] = pass_on(landed.at[k, :, 0:width], every.at[a, k], k, a)
    tail = jnp.zeros((part, 2 * hidden), jnp.float32)
    for c in range(n_ctx):
        tail = tail + landed[lax.rem(me - c + n_ctx, n_ctx), :, width:width + 2 * hidden]
    tails[0] = tail
    for a in (2, 1):
        spread[n_ctx][a] = pass_on(tails.at[0], tails.at[a], n_ctx, a)
    for k in range(n_ctx):
        spread[k][2].wait_recv()
        spread[k][3] = pass_on(every.at[2, k], every.at[3, k], k, 3)
    spread[n_ctx][2].wait_recv()
    spread[n_ctx][3] = pass_on(tails.at[2], tails.at[3], n_ctx, 3)
    for k in range(n_ctx):
        place(landed[k, :, 0:width], 0, k)
        place(every[2, k], 2, k)
        spread[k][1].wait_recv()
        place(every[1, k], 1, k)
    for k in range(n_ctx):
        spread[k][3].wait_recv()
        place(every[3, k], 3, k)
    spread[n_ctx][1].wait_recv()
    spread[n_ctx][3].wait_recv()
    for a in range(4):
        columns[rows_of[a], :] = tails[a]
    out_inner[...] = columns[0:hidden, 0:hidden]
    columns_t = columns[...].T
    out_first[...] = columns_t[hidden:hidden + w_first.shape[0], 0:hidden]
    for move in sent + moves + gathers + [move for row in spread for move in row[1:]]:
        move.wait_send()


def finish_kernel(a, b, c, out_a, out_b, out_c):
    out_a[...] = a[...]
    out_b[...] = b[...]
    out_c[...] = c[...]


def fast_shards(values, grads_out, w_first, sine_freq, w_inner, w_last, decay_rates):
    n_ctx, n_dp = lax.axis_size("ctx"), lax.axis_size("dp")
    block, channels = values.shape[1:]
    total, width = block * n_ctx, channels // n_ctx
    hidden = w_inner.shape[0]
    part = hidden // n_dp
    chunks = total // FREQ_ROWS
    scale = 1.0 / math.sqrt(values.shape[0] * n_dp * total * L)
    tables = half_step_tables(total)
    feat = feature_rows(total, hidden)
    anywhere = pl.BlockSpec(memory_space=pl.ANY)
    near = pl.BlockSpec(memory_space=pltpu.VMEM)
    f32, bf16 = jnp.float32, jnp.bfloat16
    dma = pltpu.SemaphoreType.DMA
    tail = width + 2 * hidden
    out_shape = tuple(
        jax.ShapeDtypeStruct(array.shape, f32) for array in (w_first, w_inner, w_last))
    sums = pl.pallas_call(
        functools.partial(fast_kernel, n_ctx, n_dp, scale),
        out_shape=out_shape,
        in_specs=[anywhere] * 12,
        out_specs=(near,) * 3,
        scratch_shapes=[
            pltpu.VMEM(w_first.shape, f32),
            pltpu.VMEM((1, hidden), f32),
            pltpu.VMEM(w_inner.shape, f32),
            pltpu.VMEM((hidden, width), f32),
            pltpu.VMEM((1, width), f32),
            pltpu.VMEM(feat.shape, f32),
            pltpu.VMEM((total, 2 * width), bf16),
            pltpu.VMEM(tables[0].shape, bf16),
            pltpu.VMEM(tables[1].shape, bf16),
            pltpu.VMEM(tables[2].shape, bf16),
            pltpu.VMEM(tables[3].shape, bf16),
            pltpu.VMEM((total, width), f32),
            pltpu.VMEM((2 * hidden, 2 * hidden), f32),
            pltpu.VMEM((hidden, tail), f32),
            pltpu.VMEM((n_dp, part, tail), f32),
            pltpu.VMEM((hidden, 2 * hidden), f32),
            pltpu.VMEM((n_ctx, part, tail), f32),
            pltpu.VMEM((4, n_ctx, part, width), f32),
            pltpu.VMEM((4, part, 2 * hidden), f32),
            pltpu.VMEM((chunks, 2 * FREQ_ROWS, width), f32),
            dma((10,)), dma((2,)),
            dma((2 * n_ctx,)), dma((2 * n_ctx,)),
            dma((n_dp,)), dma((n_dp,)),
            dma((n_ctx,)), dma((n_ctx,)),
            dma((4 * n_ctx + 4,)), dma((4 * n_ctx + 4,)),
        ],
        compiler_params=pltpu.CompilerParams(
            collective_id=0, has_side_effects=True, vmem_limit_bytes=VMEM_BYTES),
        name="lag_gradients",
    )(values, grads_out, *tables, w_first, sine_freq[None], w_inner, w_last,
      decay_rates[None], feat)
    return pl.pallas_call(
        finish_kernel,
        out_shape=out_shape,
        in_specs=[near] * 3,
        out_specs=(near,) * 3,
        compiler_params=pltpu.CompilerParams(vmem_limit_bytes=60 * 1024 * 1024),
        name="hand_over",
    )(*sums)


def fits_fast(mesh, values, w_inner, w_last):
    n_ctx, n_dp = mesh.shape["ctx"], mesh.shape["dp"]
    total, channels, hidden = values.shape[1], values.shape[2], w_inner.shape[0]
    return (
        n_ctx > 1 and n_dp == 4 and total <= min(L, 512) and total % FREQ_ROWS == 0
        and total // n_ctx % 16 == 0 and channels % (n_ctx * 128) == 0
        and hidden == 64 and hidden % (8 * n_dp) == 0
        and values.shape[0] == n_dp * mesh.shape["groups"]
    )


def solution(mesh):
    in_specs = (
        P(("groups", "dp"), "ctx", None),
        P(("groups", "dp"), "ctx", None),
        P(),
        P(),
        P(),
        P(),
        P(),
    )
    out_specs = (P("groups", None), P("groups", None), P("groups", None))

    def whole(values, grads_out, w_first, sine_freq, w_inner, w_last, decay_rates):
        body = fast_shards if fits_fast(mesh, values, w_inner, w_last) else shards
        return jax.shard_map(
            body, mesh=mesh, in_specs=in_specs, out_specs=out_specs, check_vma=False
        )(values, grads_out, w_first, sine_freq, w_inner, w_last, decay_rates)

    return whole
```

```python
import functools
import math

import jax
import jax.numpy as jnp
import ml_dtypes
import numpy as np
from jax import lax
from jax.experimental import pallas as pl
from jax.experimental.pallas import tpu as pltpu
from jax.sharding import PartitionSpec as P

L = 4096


HIGHEST_PREC = lax.Precision.HIGHEST


def shifted(value, axis, steps):
    count = lax.axis_size(axis)
    initial, last = (max(0, -steps), min(count, count - steps))
    return lax.ppermute(value, axis, [(source, source + steps) for source in range(initial, last)])


def position_features(row_count, lag_total):
    positions = jnp.arange(row_count, dtype=jnp.int32)
    columns = [positions.astype(jnp.float32) / lag_total]
    for band_idx in (1, 2):
        phase_idx = positions * band_idx % lag_total
        angles = 2.0 * math.pi * phase_idx.astype(jnp.float32) / lag_total
        columns.append(jnp.cos(angles))
        columns.append(jnp.sin(angles))
    return jnp.stack(columns, axis=1)


def filter_forward(features, w_first, w_inner, sine_freq):
    pre_first = jnp.dot(
        features, w_first, precision=HIGHEST_PREC, preferred_element_type=jnp.float32
    )
    act_first = jnp.sin(sine_freq * pre_first)
    pre_inner = jnp.dot(
        act_first, w_inner, precision=HIGHEST_PREC, preferred_element_type=jnp.float32
    )
    act_inner = jnp.sin(sine_freq * pre_inner)
    return (pre_first, act_first, pre_inner, act_inner)


def filter_back(features, pre_first, act_first, pre_inner, grad_act, w_inner, sine_freq):
    grad_pre = grad_act * sine_freq * jnp.cos(sine_freq * pre_inner)
    grad_inner = jnp.dot(
        act_first.T, grad_pre, precision=HIGHEST_PREC, preferred_element_type=jnp.float32
    )
    grad_act_first = jnp.dot(
        grad_pre, w_inner.T, precision=HIGHEST_PREC, preferred_element_type=jnp.float32
    )
    grad_pre_first = grad_act_first * sine_freq * jnp.cos(sine_freq * pre_first)
    grad_first = jnp.dot(
        features.T, grad_pre_first, precision=HIGHEST_PREC, preferred_element_type=jnp.float32
    )
    return (grad_first, grad_inner)


def spectral_tables(block_len):
    full_len = 2 * block_len
    freq_idx = jnp.arange(block_len, dtype=jnp.int32)
    places = jnp.arange(full_len, dtype=jnp.int32)
    phase_idx = freq_idx[:, None] * places[None, :] % full_len
    angles = math.pi * phase_idx.astype(jnp.float32) / block_len
    back_phase = freq_idx[:, None] * freq_idx[None, :] % full_len
    back_angles = math.pi * back_phase.astype(jnp.float32) / block_len
    weights = jnp.where(freq_idx == 0, 1.0, 2.0).astype(jnp.float32) / full_len
    inv_cos = jnp.cos(back_angles) * weights[None, :]
    inv_sin = jnp.sin(back_angles) * weights[None, :]
    parity = 1.0 - 2.0 * (places % 2).astype(jnp.float32)
    return (jnp.cos(angles), jnp.sin(angles), inv_cos, inv_sin, parity)


def spectrum(cos_part, sin_part, sign_part, signal):
    real_part = jnp.einsum("fn,bnc->bfc", cos_part, signal, precision=HIGHEST_PREC)
    imag_part = -jnp.einsum("fn,bnc->bfc", sin_part, signal, precision=HIGHEST_PREC)
    nyquist = jnp.einsum("n,bnc->bc", sign_part, signal, precision=HIGHEST_PREC)
    return (real_part, imag_part, nyquist)


def lag_block_update(carried, pieces, block_idx, own_spec, shared):
    grad_act, grad_last = carried
    tables, act_inner, w_last, decay_rates, grad_scale = shared
    fwd_cos, fwd_sin, inv_cos, inv_sin, parity = tables
    block_len = inv_cos.shape[0]
    blocks = act_inner.shape[0] // block_len
    own_real, own_imag, own_nyq = own_spec
    in_real, in_imag, in_nyq = spectrum(
        fwd_cos[:, block_len:],
        fwd_sin[:, block_len:],
        parity[block_len:],
        pieces.astype(jnp.float32),
    )
    cross_real = jnp.sum(in_real * own_real + in_imag * own_imag, axis=0)
    cross_imag = jnp.sum(in_imag * own_real - in_real * own_imag, axis=0)
    cross_nyq = jnp.sum(in_nyq * own_nyq, axis=0)
    lagged = jnp.dot(
        inv_cos, cross_real, precision=HIGHEST_PREC, preferred_element_type=jnp.float32
    )
    lagged = lagged - jnp.dot(
        inv_sin, cross_imag, precision=HIGHEST_PREC, preferred_element_type=jnp.float32
    )
    lagged = lagged + (parity[:block_len] / (2 * block_len))[:, None] * cross_nyq[None, :]
    in_range = (block_idx >= 0) & (block_idx < blocks)
    row_start = jnp.clip(block_idx, 0, blocks - 1) * block_len
    lag_pos = (row_start + jnp.arange(block_len, dtype=jnp.int32)).astype(jnp.float32)
    window = jnp.exp(-lag_pos[:, None] * decay_rates[None, :])
    cotangent = jnp.where(in_range, lagged * window * grad_scale, 0.0)
    act_rows = lax.dynamic_slice_in_dim(act_inner, row_start, block_len, 0)
    grad_last = grad_last + jnp.dot(
        act_rows.T, cotangent, precision=HIGHEST_PREC, preferred_element_type=jnp.float32
    )
    current = lax.dynamic_slice_in_dim(grad_act, row_start, block_len, 0)
    update = jnp.dot(
        cotangent, w_last.T, precision=HIGHEST_PREC, preferred_element_type=jnp.float32
    )
    grad_act = lax.dynamic_update_slice_in_dim(grad_act, current + update, row_start, 0)
    return (grad_act, grad_last)


def shards(values, grads_out, w_first, sine_freq, w_inner, w_last, decay_rates):
    block_len = values.shape[1]
    lag_total = L
    tables = spectral_tables(block_len)
    fwd_cos, fwd_sin, inv_cos, inv_sin, parity = tables
    token_count = (
        values.shape[0] * lax.axis_size("dp") * block_len * lax.axis_size("ctx") * lag_total
    )
    grad_scale = 1.0 / math.sqrt(token_count)
    features = position_features(lag_total, lag_total)
    pre_first, act_first, pre_inner, act_inner = filter_forward(
        features, w_first, w_inner, sine_freq
    )
    earlier = shifted(values, "ctx", 1)
    own_pair = jnp.concatenate([earlier, values], axis=1).astype(jnp.float32)
    own_spec = spectrum(fwd_cos, fwd_sin, parity, own_pair)
    shared = (tables, act_inner, w_last, decay_rates, grad_scale)
    carried = (
        jnp.zeros((lag_total, w_last.shape[0]), jnp.float32),
        jnp.zeros(w_last.shape, jnp.float32),
    )
    ctx_index = lax.axis_index("ctx")
    pieces = lax.all_gather(grads_out[None], "ctx", axis=0, tiled=True)

    def one_piece(piece_idx, piece_state):
        return lag_block_update(
            piece_state, pieces[piece_idx], piece_idx - ctx_index, own_spec, shared
        )

    carried = lax.fori_loop(0, pieces.shape[0], one_piece, carried)
    grad_act, grad_last = carried
    grad_act, grad_last = lax.psum((grad_act, grad_last), ("ctx", "dp"))
    grad_first, grad_inner = filter_back(
        features, pre_first, act_first, pre_inner, grad_act, w_inner, sine_freq
    )
    return (grad_first, grad_inner, grad_last)


MESH = pl.DeviceIdType.MESH
FREQ_ROWS = 128
VMEM_BYTES = 60 * 1024 * 1024


def split_bf16(array):
    high = array.astype(jnp.bfloat16)
    return high, (array - high.astype(jnp.float32)).astype(jnp.bfloat16)


def half_step_tables(total):
    freq = np.arange(total, dtype=np.int64)
    place = np.arange(total, dtype=np.int64)
    phase = ((2 * freq[:, None] + 1) * place[None, :]) % (4 * total)
    angle = np.pi * phase / (2 * total)
    chunks = total // FREQ_ROWS
    cos_part = np.cos(angle).reshape(chunks, FREQ_ROWS, total)
    sin_part = np.sin(angle).reshape(chunks, FREQ_ROWS, total)
    table = np.concatenate([cos_part, sin_part], axis=1).astype(np.float32)
    high = table.astype(ml_dtypes.bfloat16)
    low = (table - high.astype(np.float32)).astype(ml_dtypes.bfloat16)
    flip = lambda part: np.ascontiguousarray(part.transpose(0, 2, 1))
    return high, low, flip(high), flip(low)


def feature_rows(total, rows):
    place = np.arange(total, dtype=np.int64)
    out = np.zeros((rows, total), np.float32)
    out[0] = place / L
    for band in (1, 2):
        angle = 2.0 * np.pi * (place * band % L) / L
        out[2 * band - 1] = np.cos(angle)
        out[2 * band] = np.sin(angle)
    return out


def sin_cos(x):
    turns = jnp.floor(x * np.float32(2.0 / np.pi) + 0.5)
    r = x - turns * np.float32(1.5703125)
    r = r - turns * np.float32(4.837512969970703125e-4)
    r = r - turns * np.float32(7.54978995489188216e-8)
    z = r * r
    s = ((np.float32(-1.9515295891e-4) * z + np.float32(8.3321608736e-3)) * z
         + np.float32(-1.6666654611e-1)) * z * r + r
    c = ((np.float32(2.443315711809948e-5) * z + np.float32(-1.388731625493765e-3)) * z
         + np.float32(4.166664568298827e-2)) * z * z - 0.5 * z + 1.0
    quarter = turns - 4.0 * jnp.floor(turns * 0.25)
    odd = (quarter == 1.0) | (quarter == 3.0)
    sin_flip = jnp.where(quarter >= 2.0, -1.0, 1.0)
    cos_flip = jnp.where((quarter == 1.0) | (quarter == 2.0), -1.0, 1.0)
    return jnp.where(odd, c, s) * sin_flip, jnp.where(odd, s, c) * cos_flip


def dot(a, b, dims=((1,), (0,)), precision=None):
    return lax.dot_general(
        a, b, (dims, ((), ())), precision=precision, preferred_element_type=jnp.float32
    )


def dot_parts(a, b, dims=((1,), (0,))):
    rows = a[0].shape[0]
    first = dot(jnp.concatenate(a, axis=0), b[0], dims)
    return first[:rows] + first[rows:] + dot(a[0], b[1], dims)


def fast_kernel(
    n_ctx, n_dp, scale,
    values, grads, fhi_h, flo_h, ihi_h, ilo_h,
    w_first_h, sine_freq_h, w_inner_h, w_last_h, decay_h, feat_h,
    out_first, out_inner, out_last,
    w_first, sine_freq, w_inner, w_last, decay, feat,
    tokens, fhi, flo, ihi, ilo, window, small, partial, rx, columns, landed, every, tails, spectra,
    tab_sem, own_sem, s1, r1, s2, r2, s3, r3, s4, r4,
):
    me = lax.axis_index("ctx")
    md = lax.axis_index("dp")
    block, width = values.shape[1], values.shape[2] // n_ctx
    total = block * n_ctx
    hidden = w_inner.shape[0]
    part = hidden // n_dp

    def ctx_of(k):
        return lax.rem(me + k, n_ctx)

    def dp_of(k):
        return lax.rem(md + k, n_dp)

    barrier = pltpu.get_barrier_semaphore()
    for k in range(1, n_ctx):
        pl.semaphore_signal(
            barrier, inc=1, device_id={"ctx": ctx_of(k)}, device_id_type=MESH)
    for k in range(1, n_dp):
        pl.semaphore_signal(barrier, inc=1, device_id={"dp": dp_of(k)}, device_id_type=MESH)
    my_rows = pl.ds(pl.multiple_of(me * block, block), block)
    my_cols = pl.ds(pl.multiple_of(me * width, width), width)
    pairs = (
        (w_first_h, w_first), (sine_freq_h, sine_freq), (w_inner_h, w_inner),
        (decay_h.at[:, my_cols], decay), (feat_h, feat), (w_last_h.at[:, my_cols], w_last),
        (fhi_h, fhi), (flo_h, flo), (ihi_h, ihi), (ilo_h, ilo))
    loads = [
        pltpu.make_async_copy(src, dst, tab_sem.at[i]) for i, (src, dst) in enumerate(pairs)]
    params, tabs = loads[:6], loads[6:]
    for copy in params:
        copy.start()
    own = [
        pltpu.make_async_copy(
            src.at[0, :, my_cols], tokens.at[my_rows, pl.ds(i * width, width)], own_sem.at[i])
        for i, src in enumerate((values, grads))
    ]
    for copy in own:
        copy.start()

    pl.semaphore_wait(barrier, n_ctx + n_dp - 2)

    moves = []
    for i, src in enumerate((values, grads)):
        for k in (2, 1, 3) if n_ctx == 4 else range(1, n_ctx):
            to = ctx_of(k)
            cols = pl.ds(pl.multiple_of(to * width, width), width)
            move = pltpu.make_async_remote_copy(
                src_ref=src.at[0, :, cols],
                dst_ref=tokens.at[my_rows, pl.ds(i * width, width)],
                send_sem=s1.at[2 * k + i], recv_sem=r1.at[2 * k + i],
                device_id={"ctx": to}, device_id_type=MESH)
            move.start()
            moves.append(move)

    for copy in tabs:
        copy.start()

    for copy in params:
        copy.wait()
    small[...] = jnp.zeros_like(small)
    small[0:hidden, 0:hidden] = w_inner[...]
    small[hidden:hidden + w_first.shape[0], 0:hidden] = w_first[...]
    small[hidden + 8:hidden + 9, 0:hidden] = sine_freq[...]
    turned = small[...].T
    freq = turned[0:hidden, hidden + 8:hidden + 9]
    pre = turned[0:hidden, hidden:hidden + 1] * feat[0:1, :]
    for e in range(1, w_first.shape[0]):
        pre = pre + turned[0:hidden, hidden + e:hidden + e + 1] * feat[e:e + 1, :]
    act_first, slope_first = sin_cos(freq * pre)
    act_inner, slope_inner = sin_cos(
        freq * dot(turned[0:hidden, 0:hidden], act_first, precision=HIGHEST_PREC))
    act_inner_parts, act_first_parts = split_bf16(act_inner), split_bf16(act_first)
    w_last_parts, w_inner_parts = split_bf16(w_last[...]), split_bf16(w_inner[...])
    feat_parts = split_bf16(feat[...])
    slope_first = slope_first * freq
    slope_inner = slope_inner * freq
    lag = lax.broadcasted_iota(jnp.int32, (total, width), 0).astype(jnp.float32)
    window[...] = jnp.exp(-lag * decay[...]) * np.float32(scale / total)
    for copy in tabs + own:
        copy.wait()
    sent, moves = moves, None
    for move in sent[:n_ctx - 1]:
        move.wait_recv()
    held = tokens[:, :width]
    for i in range(total // FREQ_ROWS):
        spectra[i] = dot(fhi[i], held) + dot(flo[i], held)
    for move in sent[n_ctx - 1:]:
        move.wait_recv()

    held = tokens[:, width:]
    lagged = None
    for i in range(total // FREQ_ROWS):
        spec = dot(fhi[i], held) + dot(flo[i], held)
        v_cos, v_sin = spectra[i, :FREQ_ROWS], spectra[i, FREQ_ROWS:]
        g_cos, g_sin = spec[:FREQ_ROWS], spec[FREQ_ROWS:]
        cross = jnp.concatenate(
            [g_cos * v_cos + g_sin * v_sin, g_sin * v_cos - g_cos * v_sin], axis=0)
        high, low = split_bf16(cross)
        update = dot(ihi[i], high) + dot(ihi[i], low) + dot(ilo[i], high)
        lagged = update if lagged is None else lagged + update
    cot = split_bf16(lagged * window[...])
    across = ((1,), (1,))
    lanes = (pl.ds(0, width), pl.ds(width, 2 * hidden))
    moves, gathers = [[], []], [[], []]

    def send_rows(i):
        for k in range(1, n_dp):
            to = dp_of(k)
            move = pltpu.make_async_remote_copy(
                src_ref=partial.at[pl.ds(pl.multiple_of(to * part, part), part), lanes[i]],
                dst_ref=rx.at[k, :, lanes[i]],
                send_sem=s2.at[i * n_dp + k], recv_sem=r2.at[i * n_dp + k],
                device_id={"dp": to}, device_id_type=MESH)
            move.start()
            moves[i].append(move)

    def add_and_gather(i):
        summed = partial[pl.ds(pl.multiple_of(md * part, part), part), lanes[i]]
        for k, move in enumerate(moves[i]):
            move.wait_recv()
            summed = summed + rx[k + 1, :, lanes[i]]
        landed[0, :, lanes[i]] = summed
        for k in range(1, n_ctx):
            move = pltpu.make_async_remote_copy(
                src_ref=landed.at[0, :, lanes[i]], dst_ref=landed.at[k, :, lanes[i]],
                send_sem=s3.at[i * n_ctx + k], recv_sem=r3.at[i * n_ctx + k],
                device_id={"ctx": ctx_of(k)}, device_id_type=MESH)
            move.start()
            gathers[i].append(move)

    partial[:, 0:width] = dot_parts(act_inner_parts, cot)
    send_rows(0)
    grad_pre = dot_parts(w_last_parts, cot, across) * slope_inner
    grad_parts = split_bf16(grad_pre)
    partial[:, width:width + hidden] = dot_parts(act_first_parts, grad_parts, across)
    grad_pre_first = dot_parts(w_inner_parts, grad_parts) * slope_first
    partial[:, width + hidden:width + 2 * hidden] = dot_parts(
        split_bf16(grad_pre_first), feat_parts, across)
    send_rows(1)
    add_and_gather(0)
    add_and_gather(1)

    mate = md + 1 - 2 * lax.rem(md, 2)
    far = lax.rem(md + 2, 4)
    rows_of = [
        pl.ds(pl.multiple_of(q * part, part), part)
        for q in (md, mate, far, lax.rem(mate + 2, 4))]

    def pass_on(src, dst, k, a):
        move = pltpu.make_async_remote_copy(
            src_ref=src, dst_ref=dst, send_sem=s4.at[4 * k + a], recv_sem=r4.at[4 * k + a],
            device_id={"dp": far if a == 2 else mate}, device_id_type=MESH)
        move.start()
        return move

    def place(block, a, k):
        cols = pl.ds(pl.multiple_of(lax.rem(me - k + n_ctx, n_ctx) * width, width), width)
        out_last[rows_of[a], cols] = block

    spread = [[None] * 4 for _ in range(n_ctx + 1)]
    for k in range(n_ctx):
        if k:
            gathers[0][k - 1].wait_recv()
        for a in (2, 1):
            spread[k][a] = pass_on(landed.at[k, :, 0:width], every.at[a, k], k, a)
    for move in gathers[1]:
        move.wait_recv()
    tail = jnp.zeros((part, 2 * hidden), jnp.float32)
    for c in range(n_ctx):
        tail = tail + landed[lax.rem(me - c + n_ctx, n_ctx), :, width:width + 2 * hidden]
    tails[0] = tail
    for a in (2, 1):
        spread[n_ctx][a] = pass_on(tails.at[0], tails.at[a], n_ctx, a)
    for k in range(n_ctx):
        spread[k][2].wait_recv()
        spread[k][3] = pass_on(every.at[2, k], every.at[3, k], k, 3)
    spread[n_ctx][2].wait_recv()
    spread[n_ctx][3] = pass_on(tails.at[2], tails.at[3], n_ctx, 3)
    for k in range(n_ctx):
        place(landed[k, :, 0:width], 0, k)
        place(every[2, k], 2, k)
        spread[k][1].wait_recv()
        place(every[1, k], 1, k)
    for k in range(n_ctx):
        spread[k][3].wait_recv()
        place(every[3, k], 3, k)
    spread[n_ctx][1].wait_recv()
    spread[n_ctx][3].wait_recv()
    for a in range(4):
        columns[rows_of[a], :] = tails[a]
    out_inner[...] = columns[0:hidden, 0:hidden]
    columns_t = columns[...].T
    out_first[...] = columns_t[hidden:hidden + w_first.shape[0], 0:hidden]
    for move in sent + moves[0] + moves[1] + gathers[0] + gathers[1] + [move for row in spread for move in row[1:]]:
        move.wait_send()


def finish_kernel(a, b, c, out_a, out_b, out_c):
    out_a[...] = a[...]
    out_b[...] = b[...]
    out_c[...] = c[...]


def fast_shards(values, grads_out, w_first, sine_freq, w_inner, w_last, decay_rates):
    n_ctx, n_dp = lax.axis_size("ctx"), lax.axis_size("dp")
    block, channels = values.shape[1:]
    total, width = block * n_ctx, channels // n_ctx
    hidden = w_inner.shape[0]
    part = hidden // n_dp
    chunks = total // FREQ_ROWS
    scale = 1.0 / math.sqrt(values.shape[0] * n_dp * total * L)
    tables = half_step_tables(total)
    feat = feature_rows(total, hidden)
    anywhere = pl.BlockSpec(memory_space=pl.ANY)
    near = pl.BlockSpec(memory_space=pltpu.VMEM)
    f32, bf16 = jnp.float32, jnp.bfloat16
    dma = pltpu.SemaphoreType.DMA
    tail = width + 2 * hidden
    out_shape = tuple(
        jax.ShapeDtypeStruct(array.shape, f32) for array in (w_first, w_inner, w_last))
    sums = pl.pallas_call(
        functools.partial(fast_kernel, n_ctx, n_dp, scale),
        out_shape=out_shape,
        in_specs=[anywhere] * 12,
        out_specs=(near,) * 3,
        scratch_shapes=[
            pltpu.VMEM(w_first.shape, f32),
            pltpu.VMEM((1, hidden), f32),
            pltpu.VMEM(w_inner.shape, f32),
            pltpu.VMEM((hidden, width), f32),
            pltpu.VMEM((1, width), f32),
            pltpu.VMEM(feat.shape, f32),
            pltpu.VMEM((total, 2 * width), bf16),
            pltpu.VMEM(tables[0].shape, bf16),
            pltpu.VMEM(tables[1].shape, bf16),
            pltpu.VMEM(tables[2].shape, bf16),
            pltpu.VMEM(tables[3].shape, bf16),
            pltpu.VMEM((total, width), f32),
            pltpu.VMEM((2 * hidden, 2 * hidden), f32),
            pltpu.VMEM((hidden, tail), f32),
            pltpu.VMEM((n_dp, part, tail), f32),
            pltpu.VMEM((hidden, 2 * hidden), f32),
            pltpu.VMEM((n_ctx, part, tail), f32),
            pltpu.VMEM((4, n_ctx, part, width), f32),
            pltpu.VMEM((4, part, 2 * hidden), f32),
            pltpu.VMEM((chunks, 2 * FREQ_ROWS, width), f32),
            dma((10,)), dma((2,)),
            dma((2 * n_ctx,)), dma((2 * n_ctx,)),
            dma((2 * n_dp,)), dma((2 * n_dp,)),
            dma((2 * n_ctx,)), dma((2 * n_ctx,)),
            dma((4 * n_ctx + 4,)), dma((4 * n_ctx + 4,)),
        ],
        compiler_params=pltpu.CompilerParams(
            collective_id=0, has_side_effects=True, vmem_limit_bytes=VMEM_BYTES),
        name="lag_gradients",
    )(values, grads_out, *tables, w_first, sine_freq[None], w_inner, w_last,
      decay_rates[None], feat)
    return pl.pallas_call(
        finish_kernel,
        out_shape=out_shape,
        in_specs=[near] * 3,
        out_specs=(near,) * 3,
        compiler_params=pltpu.CompilerParams(vmem_limit_bytes=60 * 1024 * 1024),
        name="hand_over",
    )(*sums)


def fits_fast(mesh, values, w_inner, w_last):
    n_ctx, n_dp = mesh.shape["ctx"], mesh.shape["dp"]
    total, channels, hidden = values.shape[1], values.shape[2], w_inner.shape[0]
    return (
        n_ctx > 1 and n_dp == 4 and total <= min(L, 512) and total % FREQ_ROWS == 0
        and total // n_ctx % 16 == 0 and channels % (n_ctx * 128) == 0
        and hidden == 64 and hidden % (8 * n_dp) == 0
        and values.shape[0] == n_dp * mesh.shape["groups"]
    )


def solution(mesh):
    in_specs = (
        P(("groups", "dp"), "ctx", None),
        P(("groups", "dp"), "ctx", None),
        P(),
        P(),
        P(),
        P(),
        P(),
    )
    out_specs = (P("groups", None), P("groups", None), P("groups", None))

    def whole(values, grads_out, w_first, sine_freq, w_inner, w_last, decay_rates):
        body = fast_shards if fits_fast(mesh, values, w_inner, w_last) else shards
        return jax.shard_map(
            body, mesh=mesh, in_specs=in_specs, out_specs=out_specs, check_vma=False
        )(values, grads_out, w_first, sine_freq, w_inner, w_last, decay_rates)

    return whole
```

```python
import functools
import math

import jax
import jax.numpy as jnp
import ml_dtypes
import numpy as np
from jax import lax
from jax.experimental import pallas as pl
from jax.experimental.pallas import tpu as pltpu
from jax.sharding import PartitionSpec as P

L = 4096


HIGHEST_PREC = lax.Precision.HIGHEST


def shifted(value, axis, steps):
    count = lax.axis_size(axis)
    initial, last = (max(0, -steps), min(count, count - steps))
    return lax.ppermute(value, axis, [(source, source + steps) for source in range(initial, last)])


def position_features(row_count, lag_total):
    positions = jnp.arange(row_count, dtype=jnp.int32)
    columns = [positions.astype(jnp.float32) / lag_total]
    for band_idx in (1, 2):
        phase_idx = positions * band_idx % lag_total
        angles = 2.0 * math.pi * phase_idx.astype(jnp.float32) / lag_total
        columns.append(jnp.cos(angles))
        columns.append(jnp.sin(angles))
    return jnp.stack(columns, axis=1)


def filter_forward(features, w_first, w_inner, sine_freq):
    pre_first = jnp.dot(
        features, w_first, precision=HIGHEST_PREC, preferred_element_type=jnp.float32
    )
    act_first = jnp.sin(sine_freq * pre_first)
    pre_inner = jnp.dot(
        act_first, w_inner, precision=HIGHEST_PREC, preferred_element_type=jnp.float32
    )
    act_inner = jnp.sin(sine_freq * pre_inner)
    return (pre_first, act_first, pre_inner, act_inner)


def filter_back(features, pre_first, act_first, pre_inner, grad_act, w_inner, sine_freq):
    grad_pre = grad_act * sine_freq * jnp.cos(sine_freq * pre_inner)
    grad_inner = jnp.dot(
        act_first.T, grad_pre, precision=HIGHEST_PREC, preferred_element_type=jnp.float32
    )
    grad_act_first = jnp.dot(
        grad_pre, w_inner.T, precision=HIGHEST_PREC, preferred_element_type=jnp.float32
    )
    grad_pre_first = grad_act_first * sine_freq * jnp.cos(sine_freq * pre_first)
    grad_first = jnp.dot(
        features.T, grad_pre_first, precision=HIGHEST_PREC, preferred_element_type=jnp.float32
    )
    return (grad_first, grad_inner)


def spectral_tables(block_len):
    full_len = 2 * block_len
    freq_idx = jnp.arange(block_len, dtype=jnp.int32)
    places = jnp.arange(full_len, dtype=jnp.int32)
    phase_idx = freq_idx[:, None] * places[None, :] % full_len
    angles = math.pi * phase_idx.astype(jnp.float32) / block_len
    back_phase = freq_idx[:, None] * freq_idx[None, :] % full_len
    back_angles = math.pi * back_phase.astype(jnp.float32) / block_len
    weights = jnp.where(freq_idx == 0, 1.0, 2.0).astype(jnp.float32) / full_len
    inv_cos = jnp.cos(back_angles) * weights[None, :]
    inv_sin = jnp.sin(back_angles) * weights[None, :]
    parity = 1.0 - 2.0 * (places % 2).astype(jnp.float32)
    return (jnp.cos(angles), jnp.sin(angles), inv_cos, inv_sin, parity)


def spectrum(cos_part, sin_part, sign_part, signal):
    real_part = jnp.einsum("fn,bnc->bfc", cos_part, signal, precision=HIGHEST_PREC)
    imag_part = -jnp.einsum("fn,bnc->bfc", sin_part, signal, precision=HIGHEST_PREC)
    nyquist = jnp.einsum("n,bnc->bc", sign_part, signal, precision=HIGHEST_PREC)
    return (real_part, imag_part, nyquist)


def lag_block_update(carried, pieces, block_idx, own_spec, shared):
    grad_act, grad_last = carried
    tables, act_inner, w_last, decay_rates, grad_scale = shared
    fwd_cos, fwd_sin, inv_cos, inv_sin, parity = tables
    block_len = inv_cos.shape[0]
    blocks = act_inner.shape[0] // block_len
    own_real, own_imag, own_nyq = own_spec
    in_real, in_imag, in_nyq = spectrum(
        fwd_cos[:, block_len:],
        fwd_sin[:, block_len:],
        parity[block_len:],
        pieces.astype(jnp.float32),
    )
    cross_real = jnp.sum(in_real * own_real + in_imag * own_imag, axis=0)
    cross_imag = jnp.sum(in_imag * own_real - in_real * own_imag, axis=0)
    cross_nyq = jnp.sum(in_nyq * own_nyq, axis=0)
    lagged = jnp.dot(
        inv_cos, cross_real, precision=HIGHEST_PREC, preferred_element_type=jnp.float32
    )
    lagged = lagged - jnp.dot(
        inv_sin, cross_imag, precision=HIGHEST_PREC, preferred_element_type=jnp.float32
    )
    lagged = lagged + (parity[:block_len] / (2 * block_len))[:, None] * cross_nyq[None, :]
    in_range = (block_idx >= 0) & (block_idx < blocks)
    row_start = jnp.clip(block_idx, 0, blocks - 1) * block_len
    lag_pos = (row_start + jnp.arange(block_len, dtype=jnp.int32)).astype(jnp.float32)
    window = jnp.exp(-lag_pos[:, None] * decay_rates[None, :])
    cotangent = jnp.where(in_range, lagged * window * grad_scale, 0.0)
    act_rows = lax.dynamic_slice_in_dim(act_inner, row_start, block_len, 0)
    grad_last = grad_last + jnp.dot(
        act_rows.T, cotangent, precision=HIGHEST_PREC, preferred_element_type=jnp.float32
    )
    current = lax.dynamic_slice_in_dim(grad_act, row_start, block_len, 0)
    update = jnp.dot(
        cotangent, w_last.T, precision=HIGHEST_PREC, preferred_element_type=jnp.float32
    )
    grad_act = lax.dynamic_update_slice_in_dim(grad_act, current + update, row_start, 0)
    return (grad_act, grad_last)


def shards(values, grads_out, w_first, sine_freq, w_inner, w_last, decay_rates):
    block_len = values.shape[1]
    lag_total = L
    tables = spectral_tables(block_len)
    fwd_cos, fwd_sin, inv_cos, inv_sin, parity = tables
    token_count = (
        values.shape[0] * lax.axis_size("dp") * block_len * lax.axis_size("ctx") * lag_total
    )
    grad_scale = 1.0 / math.sqrt(token_count)
    features = position_features(lag_total, lag_total)
    pre_first, act_first, pre_inner, act_inner = filter_forward(
        features, w_first, w_inner, sine_freq
    )
    earlier = shifted(values, "ctx", 1)
    own_pair = jnp.concatenate([earlier, values], axis=1).astype(jnp.float32)
    own_spec = spectrum(fwd_cos, fwd_sin, parity, own_pair)
    shared = (tables, act_inner, w_last, decay_rates, grad_scale)
    carried = (
        jnp.zeros((lag_total, w_last.shape[0]), jnp.float32),
        jnp.zeros(w_last.shape, jnp.float32),
    )
    ctx_index = lax.axis_index("ctx")
    pieces = lax.all_gather(grads_out[None], "ctx", axis=0, tiled=True)

    def one_piece(piece_idx, piece_state):
        return lag_block_update(
            piece_state, pieces[piece_idx], piece_idx - ctx_index, own_spec, shared
        )

    carried = lax.fori_loop(0, pieces.shape[0], one_piece, carried)
    grad_act, grad_last = carried
    grad_act, grad_last = lax.psum((grad_act, grad_last), ("ctx", "dp"))
    grad_first, grad_inner = filter_back(
        features, pre_first, act_first, pre_inner, grad_act, w_inner, sine_freq
    )
    return (grad_first, grad_inner, grad_last)


MESH = pl.DeviceIdType.MESH
FREQ_ROWS = 128
VMEM_BYTES = 60 * 1024 * 1024


def split_bf16(array):
    high = array.astype(jnp.bfloat16)
    return high, (array - high.astype(jnp.float32)).astype(jnp.bfloat16)


def half_step_tables(total):
    freq = np.arange(total, dtype=np.int64)
    place = np.arange(total, dtype=np.int64)
    phase = ((2 * freq[:, None] + 1) * place[None, :]) % (4 * total)
    angle = np.pi * phase / (2 * total)
    chunks = total // FREQ_ROWS
    cos_part = np.cos(angle).reshape(chunks, FREQ_ROWS, total)
    sin_part = np.sin(angle).reshape(chunks, FREQ_ROWS, total)
    table = np.concatenate([cos_part, sin_part], axis=1).astype(np.float32)
    high = table.astype(ml_dtypes.bfloat16)
    low = (table - high.astype(np.float32)).astype(ml_dtypes.bfloat16)
    flip = lambda part: np.ascontiguousarray(part.transpose(0, 2, 1))
    return high, low, flip(high), flip(low)


def feature_rows(total, rows):
    place = np.arange(total, dtype=np.int64)
    out = np.zeros((rows, total), np.float32)
    out[0] = place / L
    for band in (1, 2):
        angle = 2.0 * np.pi * (place * band % L) / L
        out[2 * band - 1] = np.cos(angle)
        out[2 * band] = np.sin(angle)
    return out


def sin_cos(x):
    turns = jnp.floor(x * np.float32(2.0 / np.pi) + 0.5)
    r = x - turns * np.float32(1.5703125)
    r = r - turns * np.float32(4.837512969970703125e-4)
    r = r - turns * np.float32(7.54978995489188216e-8)
    z = r * r
    s = ((np.float32(-1.9515295891e-4) * z + np.float32(8.3321608736e-3)) * z
         + np.float32(-1.6666654611e-1)) * z * r + r
    c = ((np.float32(2.443315711809948e-5) * z + np.float32(-1.388731625493765e-3)) * z
         + np.float32(4.166664568298827e-2)) * z * z - 0.5 * z + 1.0
    quarter = turns - 4.0 * jnp.floor(turns * 0.25)
    odd = (quarter == 1.0) | (quarter == 3.0)
    sin_flip = jnp.where(quarter >= 2.0, -1.0, 1.0)
    cos_flip = jnp.where((quarter == 1.0) | (quarter == 2.0), -1.0, 1.0)
    return jnp.where(odd, c, s) * sin_flip, jnp.where(odd, s, c) * cos_flip


def dot(a, b, dims=((1,), (0,)), precision=None):
    return lax.dot_general(
        a, b, (dims, ((), ())), precision=precision, preferred_element_type=jnp.float32
    )


def dot_parts(a, b, dims=((1,), (0,))):
    rows = a[0].shape[0]
    first = dot(jnp.concatenate(a, axis=0), b[0], dims)
    return first[:rows] + first[rows:] + dot(a[0], b[1], dims)


def fast_kernel(
    n_ctx, n_dp, scale,
    values, grads, fhi_h, flo_h, ihi_h, ilo_h,
    w_first_h, sine_freq_h, w_inner_h, w_last_h, decay_h, feat_h,
    out_first, out_inner, out_last,
    w_first, sine_freq, w_inner, w_last, decay, feat,
    tokens, fhi, flo, ihi, ilo, window, small, partial, rx, columns, landed, every, tails, spectra,
    tab_sem, own_sem, s1, r1, s2, r2, s3, r3, s4, r4,
):
    me = lax.axis_index("ctx")
    md = lax.axis_index("dp")
    block, width = values.shape[1], values.shape[2] // n_ctx
    total = block * n_ctx
    hidden = w_inner.shape[0]
    part = hidden // n_dp

    def ctx_of(k):
        return lax.rem(me + k, n_ctx)

    def dp_of(k):
        return lax.rem(md + k, n_dp)

    barrier = pltpu.get_barrier_semaphore()
    for k in range(1, n_ctx):
        pl.semaphore_signal(
            barrier, inc=1, device_id={"ctx": ctx_of(k)}, device_id_type=MESH)
    for k in range(1, n_dp):
        pl.semaphore_signal(barrier, inc=1, device_id={"dp": dp_of(k)}, device_id_type=MESH)
    my_rows = pl.ds(pl.multiple_of(me * block, block), block)
    my_cols = pl.ds(pl.multiple_of(me * width, width), width)
    pairs = (
        (w_first_h, w_first), (sine_freq_h, sine_freq), (w_inner_h, w_inner),
        (decay_h.at[:, my_cols], decay), (feat_h, feat), (w_last_h.at[:, my_cols], w_last),
        (fhi_h, fhi), (flo_h, flo), (ihi_h, ihi), (ilo_h, ilo))
    loads = [
        pltpu.make_async_copy(src, dst, tab_sem.at[i]) for i, (src, dst) in enumerate(pairs)]
    params, tabs = loads[:6], loads[6:]
    for copy in params:
        copy.start()
    own = [
        pltpu.make_async_copy(
            src.at[0, :, my_cols], tokens.at[my_rows, pl.ds(i * width, width)], own_sem.at[i])
        for i, src in enumerate((values, grads))
    ]
    for copy in own:
        copy.start()

    pl.semaphore_wait(barrier, n_ctx + n_dp - 2)

    moves = []
    for i, src in enumerate((values, grads)):
        for k in (2, 1, 3) if n_ctx == 4 else range(1, n_ctx):
            to = ctx_of(k)
            cols = pl.ds(pl.multiple_of(to * width, width), width)
            move = pltpu.make_async_remote_copy(
                src_ref=src.at[0, :, cols],
                dst_ref=tokens.at[my_rows, pl.ds(i * width, width)],
                send_sem=s1.at[2 * k + i], recv_sem=r1.at[2 * k + i],
                device_id={"ctx": to}, device_id_type=MESH)
            move.start()
            moves.append(move)

    for copy in tabs:
        copy.start()

    for copy in params:
        copy.wait()
    small[...] = jnp.zeros_like(small)
    small[0:hidden, 0:hidden] = w_inner[...]
    small[hidden:hidden + w_first.shape[0], 0:hidden] = w_first[...]
    small[hidden + 8:hidden + 9, 0:hidden] = sine_freq[...]
    turned = small[...].T
    freq = turned[0:hidden, hidden + 8:hidden + 9]
    pre = turned[0:hidden, hidden:hidden + 1] * feat[0:1, :]
    for e in range(1, w_first.shape[0]):
        pre = pre + turned[0:hidden, hidden + e:hidden + e + 1] * feat[e:e + 1, :]
    act_first, slope_first = sin_cos(freq * pre)
    act_inner, slope_inner = sin_cos(
        freq * dot(turned[0:hidden, 0:hidden], act_first, precision=HIGHEST_PREC))
    act_inner_parts, act_first_parts = split_bf16(act_inner), split_bf16(act_first)
    w_last_parts, w_inner_parts = split_bf16(w_last[...]), split_bf16(w_inner[...])
    feat_parts = split_bf16(feat[...])
    slope_first = slope_first * freq
    slope_inner = slope_inner * freq
    lag = lax.broadcasted_iota(jnp.int32, (total, width), 0).astype(jnp.float32)
    window[...] = jnp.exp(-lag * decay[...]) * np.float32(scale / total)
    for copy in tabs + own:
        copy.wait()
    sent, moves = moves, None
    for move in sent[:n_ctx - 1]:
        move.wait_recv()
    held = tokens[:, :width]
    for i in range(total // FREQ_ROWS):
        spectra[i] = dot(fhi[i], held) + dot(flo[i], held)
    for move in sent[n_ctx - 1:]:
        move.wait_recv()

    held = tokens[:, width:]
    lagged = None
    for i in range(total // FREQ_ROWS):
        spec = dot(fhi[i], held) + dot(flo[i], held)
        v_cos, v_sin = spectra[i, :FREQ_ROWS], spectra[i, FREQ_ROWS:]
        g_cos, g_sin = spec[:FREQ_ROWS], spec[FREQ_ROWS:]
        cross = jnp.concatenate(
            [g_cos * v_cos + g_sin * v_sin, g_sin * v_cos - g_cos * v_sin], axis=0)
        high, low = split_bf16(cross)
        update = dot(ihi[i], high) + dot(ihi[i], low) + dot(ilo[i], high)
        lagged = update if lagged is None else lagged + update
    cot = split_bf16(lagged * window[...])
    across = ((1,), (1,))
    lanes = (pl.ds(0, width), pl.ds(width, 2 * hidden))
    moves, gathers = [[], []], [[], []]

    def send_rows(i):
        for k in range(1, n_dp):
            to = dp_of(k)
            move = pltpu.make_async_remote_copy(
                src_ref=partial.at[pl.ds(pl.multiple_of(to * part, part), part), lanes[i]],
                dst_ref=rx.at[k, :, lanes[i]],
                send_sem=s2.at[i * n_dp + k], recv_sem=r2.at[i * n_dp + k],
                device_id={"dp": to}, device_id_type=MESH)
            move.start()
            moves[i].append(move)

    def add_and_gather(i):
        summed = partial[pl.ds(pl.multiple_of(md * part, part), part), lanes[i]]
        for k, move in enumerate(moves[i]):
            move.wait_recv()
            summed = summed + rx[k + 1, :, lanes[i]]
        landed[0, :, lanes[i]] = summed
        for k in range(1, n_ctx):
            move = pltpu.make_async_remote_copy(
                src_ref=landed.at[0, :, lanes[i]], dst_ref=landed.at[k, :, lanes[i]],
                send_sem=s3.at[i * n_ctx + k], recv_sem=r3.at[i * n_ctx + k],
                device_id={"ctx": ctx_of(k)}, device_id_type=MESH)
            move.start()
            gathers[i].append(move)

    partial[:, 0:width] = dot_parts(act_inner_parts, cot)
    send_rows(0)
    grad_pre = dot_parts(w_last_parts, cot, across) * slope_inner
    grad_parts = split_bf16(grad_pre)
    partial[:, width:width + hidden] = dot_parts(act_first_parts, grad_parts, across)
    grad_pre_first = dot_parts(w_inner_parts, grad_parts) * slope_first
    partial[:, width + hidden:width + 2 * hidden] = dot_parts(
        split_bf16(grad_pre_first), feat_parts, across)
    send_rows(1)
    add_and_gather(0)
    add_and_gather(1)

    mate = md + 1 - 2 * lax.rem(md, 2)
    far = lax.rem(md + 2, 4)
    rows_of = [
        pl.ds(pl.multiple_of(q * part, part), part)
        for q in (md, mate, far, lax.rem(mate + 2, 4))]

    def pass_on(src, dst, k, a):
        move = pltpu.make_async_remote_copy(
            src_ref=src, dst_ref=dst, send_sem=s4.at[4 * k + a], recv_sem=r4.at[4 * k + a],
            device_id={"dp": (md, mate, far, lax.rem(mate + 2, 4))[a]}, device_id_type=MESH)
        move.start()
        return move

    def place(block, a, k):
        cols = pl.ds(pl.multiple_of(lax.rem(me - k + n_ctx, n_ctx) * width, width), width)
        out_last[rows_of[a], cols] = block

    spread = [[None] * 4 for _ in range(n_ctx + 1)]
    for k in range(n_ctx):
        if k:
            gathers[0][k - 1].wait_recv()
        for a in (3, 2, 1):
            spread[k][a] = pass_on(landed.at[k, :, 0:width], every.at[a, k], k, a)
    for move in gathers[1]:
        move.wait_recv()
    tail = jnp.zeros((part, 2 * hidden), jnp.float32)
    for c in range(n_ctx):
        tail = tail + landed[lax.rem(me - c + n_ctx, n_ctx), :, width:width + 2 * hidden]
    tails[0] = tail
    for a in (3, 2, 1):
        spread[n_ctx][a] = pass_on(tails.at[0], tails.at[a], n_ctx, a)
    for k in range(n_ctx):
        place(landed[k, :, 0:width], 0, k)
        spread[k][2].wait_recv()
        place(every[2, k], 2, k)
        spread[k][1].wait_recv()
        place(every[1, k], 1, k)
    for k in range(n_ctx):
        spread[k][3].wait_recv()
        place(every[3, k], 3, k)
    spread[n_ctx][1].wait_recv()
    spread[n_ctx][2].wait_recv()
    spread[n_ctx][3].wait_recv()
    for a in range(4):
        columns[rows_of[a], :] = tails[a]
    out_inner[...] = columns[0:hidden, 0:hidden]
    columns_t = columns[...].T
    out_first[...] = columns_t[hidden:hidden + w_first.shape[0], 0:hidden]
    for move in sent + moves[0] + moves[1] + gathers[0] + gathers[1] + [move for row in spread for move in row[1:]]:
        move.wait_send()


def finish_kernel(a, b, c, out_a, out_b, out_c):
    out_a[...] = a[...]
    out_b[...] = b[...]
    out_c[...] = c[...]


def fast_shards(values, grads_out, w_first, sine_freq, w_inner, w_last, decay_rates):
    n_ctx, n_dp = lax.axis_size("ctx"), lax.axis_size("dp")
    block, channels = values.shape[1:]
    total, width = block * n_ctx, channels // n_ctx
    hidden = w_inner.shape[0]
    part = hidden // n_dp
    chunks = total // FREQ_ROWS
    scale = 1.0 / math.sqrt(values.shape[0] * n_dp * total * L)
    tables = half_step_tables(total)
    feat = feature_rows(total, hidden)
    anywhere = pl.BlockSpec(memory_space=pl.ANY)
    near = pl.BlockSpec(memory_space=pltpu.VMEM)
    f32, bf16 = jnp.float32, jnp.bfloat16
    dma = pltpu.SemaphoreType.DMA
    tail = width + 2 * hidden
    out_shape = tuple(
        jax.ShapeDtypeStruct(array.shape, f32) for array in (w_first, w_inner, w_last))
    sums = pl.pallas_call(
        functools.partial(fast_kernel, n_ctx, n_dp, scale),
        out_shape=out_shape,
        in_specs=[anywhere] * 12,
        out_specs=(near,) * 3,
        scratch_shapes=[
            pltpu.VMEM(w_first.shape, f32),
            pltpu.VMEM((1, hidden), f32),
            pltpu.VMEM(w_inner.shape, f32),
            pltpu.VMEM((hidden, width), f32),
            pltpu.VMEM((1, width), f32),
            pltpu.VMEM(feat.shape, f32),
            pltpu.VMEM((total, 2 * width), bf16),
            pltpu.VMEM(tables[0].shape, bf16),
            pltpu.VMEM(tables[1].shape, bf16),
            pltpu.VMEM(tables[2].shape, bf16),
            pltpu.VMEM(tables[3].shape, bf16),
            pltpu.VMEM((total, width), f32),
            pltpu.VMEM((2 * hidden, 2 * hidden), f32),
            pltpu.VMEM((hidden, tail), f32),
            pltpu.VMEM((n_dp, part, tail), f32),
            pltpu.VMEM((hidden, 2 * hidden), f32),
            pltpu.VMEM((n_ctx, part, tail), f32),
            pltpu.VMEM((4, n_ctx, part, width), f32),
            pltpu.VMEM((4, part, 2 * hidden), f32),
            pltpu.VMEM((chunks, 2 * FREQ_ROWS, width), f32),
            dma((10,)), dma((2,)),
            dma((2 * n_ctx,)), dma((2 * n_ctx,)),
            dma((2 * n_dp,)), dma((2 * n_dp,)),
            dma((2 * n_ctx,)), dma((2 * n_ctx,)),
            dma((4 * n_ctx + 4,)), dma((4 * n_ctx + 4,)),
        ],
        compiler_params=pltpu.CompilerParams(
            collective_id=0, has_side_effects=True, vmem_limit_bytes=VMEM_BYTES),
        name="lag_gradients",
    )(values, grads_out, *tables, w_first, sine_freq[None], w_inner, w_last,
      decay_rates[None], feat)
    return pl.pallas_call(
        finish_kernel,
        out_shape=out_shape,
        in_specs=[near] * 3,
        out_specs=(near,) * 3,
        compiler_params=pltpu.CompilerParams(vmem_limit_bytes=60 * 1024 * 1024),
        name="hand_over",
    )(*sums)


def fits_fast(mesh, values, w_inner, w_last):
    n_ctx, n_dp = mesh.shape["ctx"], mesh.shape["dp"]
    total, channels, hidden = values.shape[1], values.shape[2], w_inner.shape[0]
    return (
        n_ctx > 1 and n_dp == 4 and total <= min(L, 512) and total % FREQ_ROWS == 0
        and total // n_ctx % 16 == 0 and channels % (n_ctx * 128) == 0
        and hidden == 64 and hidden % (8 * n_dp) == 0
        and values.shape[0] == n_dp * mesh.shape["groups"]
    )


def solution(mesh):
    in_specs = (
        P(("groups", "dp"), "ctx", None),
        P(("groups", "dp"), "ctx", None),
        P(),
        P(),
        P(),
        P(),
        P(),
    )
    out_specs = (P("groups", None), P("groups", None), P("groups", None))

    def whole(values, grads_out, w_first, sine_freq, w_inner, w_last, decay_rates):
        body = fast_shards if fits_fast(mesh, values, w_inner, w_last) else shards
        return jax.shard_map(
            body, mesh=mesh, in_specs=in_specs, out_specs=out_specs, check_vma=False
        )(values, grads_out, w_first, sine_freq, w_inner, w_last, decay_rates)

    return whole
```
